128 devices in a mesh: dp: 16 (over x, y), ctx: 8 (over z, core).
Axes of the slice: x: 4, y: 4, z: 4, core: 2. Of those that a mesh axis runs over, the one named last changes fastest.
Arguments:
- queries: bfloat16 [24576, 4096], P(('dp', 'ctx'))
- keys: bfloat16 [24576, 512], P(('dp', 'ctx'))
- values: bfloat16 [24576, 512], P(('dp', 'ctx')), may hold values from -6 to 6
- grad_out: bfloat16 [24576, 4096], P(('dp', 'ctx')), may hold values from -6 to 6
- destination: int32 [24576], P(('dp', 'ctx')), may hold values from 0 to 24575, as said below
- lengths: int32 [16, 2], replicated, may hold values from 1 to 1024, 1536 in all within a row
Outputs:
- attended: bfloat16 [24576, 4096], P(('dp', 'ctx'))
- grad_queries: bfloat16 [24576, 4096], P(('dp', 'ctx'))
- grad_keys: bfloat16 [24576, 512], P(('dp', 'ctx'))
- grad_values: bfloat16 [24576, 512], P(('dp', 'ctx'))
The draws below stay inside these ranges and needn't reach their ends.
Inputs may be any that keep to these rules, and one draw needn't show every extreme that they name: destination is a permutation of all rows; a row keeps its index of ctx; every device of a group receives exactly 192 rows; the rows of one device going to one index of dp number at most 24, and that many in every draw. Each group's lengths sum to 1536.
All inputs are finite; a program needn't handle non-finite values.
Results may differ from the reference program's by a relative error of at most 0.012.
The reference program's roundings to bfloat16 on the way (of `prob_b` and `dscore_b`) count: a program that leaves them out, or rounds other values in their place, can miss the bound.
Values may be sent and summed in bfloat16 or wider, within the bound.
A program may use at most 256 MiB of HBM per device.

```python
import math
import jax
import jax.numpy as jnp
import numpy as np
from jax import lax

D_HEAD = 128
HEADS = 32
KV_HEADS = 4
TOK_DEV = 192
SEQS = 2
CAP = 24
GROUP_ROWS = 1536
TOKENS = 24576
N_DP = 16
N_CTX = 8


def query_base(key):
    return jax.random.normal(key, (TOKENS, HEADS * D_HEAD), jnp.float32)


def draw_queries(key, part):
    base = query_base(key)
    return base.astype(jnp.bfloat16)


def draw_keys(key, part):
    key = jax.random.fold_in(key, 7)
    own = jax.random.normal(key, (TOKENS, KV_HEADS * D_HEAD), jnp.float32)
    return own.astype(jnp.bfloat16)


def draw_destination(key, part):
    key = jax.random.fold_in(key, 11)
    keys_all = jax.random.split(key, 4)
    sigma = jax.vmap(lambda kk: jax.random.permutation(kk, N_DP))(jax.random.split(keys_all[0], N_CTX))
    ranked = jax.vmap(lambda kk: jax.random.permutation(kk, N_DP))(jax.random.split(keys_all[1], N_CTX))
    half = N_DP // 2
    weight = jnp.where(ranked < half - 2, CAP, jnp.where(ranked < half + 2, CAP // 2, 0))
    offset = jnp.cumsum(weight, axis=1) - weight
    spot = jnp.arange(TOK_DEV)
    inside = (spot[None, :, None] >= offset[:, None, :]) & (spot[None, :, None] < (offset + weight)[:, None, :])
    shift = jnp.sum(inside.astype(jnp.int32) * jnp.arange(N_DP)[None, None, :], axis=2)
    source_dev = jnp.arange(N_DP)
    position = (source_dev[:, None, None] + shift[None, :, :]) % N_DP
    target = jnp.take_along_axis(jnp.broadcast_to(sigma[None], (N_DP, N_CTX, N_DP)), position, axis=2)
    slot_perm = jax.vmap(lambda kk: jax.random.permutation(kk, TOK_DEV))(jax.random.split(keys_all[2], N_DP * N_CTX)).reshape(N_DP, N_CTX, TOK_DEV)
    column = jnp.arange(N_CTX)[None, :, None]
    slot = slot_perm[target, column, spot[None, None, :]]
    dest = (target * N_CTX + column) * TOK_DEV + slot
    row_perm = jax.vmap(lambda kk: jax.random.permutation(kk, TOK_DEV))(jax.random.split(keys_all[3], N_DP * N_CTX)).reshape(N_DP, N_CTX, TOK_DEV)
    dev_index = jnp.broadcast_to(source_dev[:, None, None], dest.shape)
    col_index = jnp.broadcast_to(column, dest.shape)
    placed = jnp.zeros_like(dest).at[dev_index, col_index, row_perm].set(dest)
    return placed.reshape(-1).astype(jnp.int32)


def block_levels(own_key, extent, pieces, least, high):
    def one(dim, parts):
        heights = jax.random.uniform(jax.random.fold_in(jax.random.fold_in(own_key, 6), dim), (parts,), jnp.float32, least / len(pieces), high / len(pieces))
        return jnp.repeat(jnp.exp(heights), extent[dim] // parts).reshape((-1,) + (1,) * (len(extent) - dim - 1))

    level = one(*pieces[0])
    for cut in pieces[1:]:
        level = level * one(*cut)
    return level


def profile(count, total, bound, skew):
    weights = [(1 << 20) // math.isqrt(grade ** skew) + 1 for grade in range(2, count + 1)]
    spare, holding = total - bound - (count - 1), [1] * (count - 1)
    while spare > 0:
        free = [i for i in range(count - 1) if holding[i] < bound]
        whole, left = sum([weights[i] for i in free]), spare
        for i in free:
            addition = min(bound - holding[i], max(1, left * weights[i] // whole), spare)
            holding[i] = holding[i] + addition
            spare = spare - addition
    return np.array([bound] + holding)


def uneven_parts(rng, number_of, total, most, lean):
    if number_of == 2:
        one = jax.random.randint(rng, (), max(1, total - most), min(most, total - 1) + 1)
        return jnp.stack([one, total - one])
    tallies = jnp.asarray(profile(number_of, total, most, lean), jnp.int32)
    couples = (number_of - 1) // 2
    giver, receiver = tallies[1:1 + 2 * couples:2], tallies[2:2 + 2 * couples:2]
    room = jnp.minimum(giver - 1, most - receiver)
    moved = jax.random.randint(jax.random.fold_in(rng, 1), (couples,), 0, 1 << 20) % (room + 1)
    tallies = tallies.at[1:1 + 2 * couples:2].set(giver - moved).at[2:2 + 2 * couples:2].set(receiver + moved)
    return tallies[jax.random.permutation(jax.random.fold_in(rng, 2), number_of)]


def bell_draw(key, dims, scale, reach, cuts=(), held_as=jnp.bfloat16):
    result = jax.random.normal(key, dims, jnp.float32) * scale
    if len(cuts) > 0:
        result = block_levels(key, dims, cuts, -0.22, 0.18) * result
    return jnp.clip(result, min=-reach, max=reach).astype(held_as)


def setup_inputs(seed: int = 0) -> dict:
    seeds = jax.random.split(jax.random.key(seed), 7)
    queries = draw_queries(jax.random.fold_in(seeds[6], 71), 0)
    keys = draw_keys(jax.random.fold_in(seeds[6], 71), 0)
    values = bell_draw(seeds[2], (TOKENS, KV_HEADS * D_HEAD), 1.0, 6.0, ((0, 128),))
    grad_out = bell_draw(seeds[3], (TOKENS, HEADS * D_HEAD), 1.0, 6.0, ((0, 128),))
    destination = draw_destination(jax.random.fold_in(seeds[6], 71), 0)
    lengths = jax.vmap(lambda own: uneven_parts(own, SEQS, GROUP_ROWS, GROUP_ROWS * 2 // 3, 1))(jax.random.split(seeds[5], N_DP)).reshape((N_DP, SEQS)).astype(jnp.int32)
    return dict(queries=queries, keys=keys, values=values, grad_out=grad_out, destination=destination, lengths=lengths)


def group_attention(q_rows, k_rows, v_rows, d_rows, seq_len):
    rows = q_rows.shape[0]
    ratio = HEADS // KV_HEADS
    scale = 1.0 / (D_HEAD ** 0.5)
    ends = jnp.cumsum(seq_len)
    where_row = jnp.arange(rows, dtype=jnp.int32)
    segment = jnp.sum((where_row[:, None] >= ends[None, :]).astype(jnp.int32), axis=1)
    allowed = (segment[:, None] == segment[None, :]) & (where_row[:, None] >= where_row[None, :])
    qh = jnp.transpose(q_rows.reshape(rows, KV_HEADS, ratio, D_HEAD).astype(jnp.float32), (1, 0, 2, 3))
    kh = jnp.transpose(k_rows.reshape(rows, KV_HEADS, D_HEAD).astype(jnp.float32), (1, 0, 2))
    vh = jnp.transpose(v_rows.reshape(rows, KV_HEADS, D_HEAD).astype(jnp.float32), (1, 0, 2))
    dh = jnp.transpose(d_rows.reshape(rows, KV_HEADS, ratio, D_HEAD).astype(jnp.float32), (1, 0, 2, 3))

    def head_group(items):
        q_one, k_one, v_one, d_one = items
        scores = jnp.einsum('qrd,kd->rqk', q_one, k_one) * scale
        masked = jnp.where(allowed[None], scores, -jnp.inf)
        top = jnp.max(masked, axis=-1, keepdims=True)
        expo = jnp.exp(masked - top)
        prob = expo / jnp.sum(expo, axis=-1, keepdims=True)
        prob_b = prob.astype(jnp.bfloat16).astype(jnp.float32)
        attended = jnp.einsum('rqk,kd->qrd', prob_b, v_one).astype(jnp.bfloat16)
        delta = jnp.sum(d_one * attended.astype(jnp.float32), axis=-1)
        dprob = jnp.einsum('qrd,kd->rqk', d_one, v_one)
        dscore = prob * (dprob - jnp.transpose(delta, (1, 0))[..., None])
        dscore_b = dscore.astype(jnp.bfloat16).astype(jnp.float32)
        grad_q = (jnp.einsum('rqk,kd->qrd', dscore_b, k_one) * scale).astype(jnp.bfloat16)
        grad_k = (jnp.einsum('rqk,qrd->kd', dscore_b, q_one) * scale).astype(jnp.bfloat16)
        grad_v = jnp.einsum('rqk,qrd->kd', prob_b, d_one).astype(jnp.bfloat16)
        return attended, grad_q, grad_k, grad_v

    att, gq, gk, gv = lax.map(head_group, (qh, kh, vh, dh))
    att = jnp.transpose(att, (1, 0, 2, 3)).reshape(rows, -1)
    gq = jnp.transpose(gq, (1, 0, 2, 3)).reshape(rows, -1)
    gk = jnp.transpose(gk, (1, 0, 2)).reshape(rows, -1)
    gv = jnp.transpose(gv, (1, 0, 2)).reshape(rows, -1)
    return att, gq, gk, gv


def reference(queries, keys, values, grad_out, destination, lengths):
    def regroup(x):
        return jnp.zeros_like(x).at[destination].set(x).reshape(N_DP, TOK_DEV * N_CTX, x.shape[1])

    def one_group(items):
        return group_attention(*items)

    results = lax.map(one_group, (regroup(queries), regroup(keys), regroup(values), regroup(grad_out), lengths))

    def give_back(y):
        return y.reshape(TOKENS, -1)[destination]

    return (give_back(results[0]), give_back(results[1]), give_back(results[2]), give_back(results[3]))
```

```python
import functools
import math

import jax
import jax.numpy as jnp
from jax import lax
from jax.experimental import pallas as pl
from jax.experimental.pallas import tpu as pltpu
from jax.sharding import PartitionSpec as P

D = 128
TOK = 192
CAP = 24
F32 = jnp.float32
BF16 = jnp.bfloat16
MESH = pl.DeviceIdType.MESH
VMEM = pl.BlockSpec(memory_space=pltpu.VMEM)
SMEM = pl.BlockSpec(memory_space=pltpu.SMEM)
ANY = pl.BlockSpec(memory_space=pl.ANY)
DMA = pltpu.SemaphoreType.DMA
NN = (((1,), (0,)), ((), ()))
NT = (((1,), (1,)), ((), ()))
TN = (((0,), (0,)), ((), ()))
TILE = 256
SCALE = 1.0 / math.sqrt(D)
EXP2 = SCALE * math.log2(math.e)


def dot(a, b, dims=NN):
    return lax.dot_general(a, b, dims, preferred_element_type=F32)


def iota(shape, axis):
    return lax.broadcasted_iota(jnp.int32, shape, axis)


def group_of(dest):
    return ((dest >> 9) * 43) >> 7


def place_of(dest):
    return dest - 192 * (((dest >> 6) * 171) >> 9)


NEAR = [(dx, dy) for dx in (-1, 0, 1) for dy in (-1, 0, 1) if (dx, dy) != (0, 0)]
FAR = [(2, 0), (2, 1), (2, -1), (0, 2), (1, 2), (-1, 2), (2, 2)]


class Here:
    def __init__(self):
        self.dp = lax.axis_index("dp")
        self.ctx = lax.axis_index("ctx")
        self.x, self.y = self.dp // 4, self.dp % 4

    def at(self, dx, dy):
        return ((self.x + (dx + 4)) % 4) * 4 + (self.y + (dy + 4)) % 4

    def peer(self, step):
        return (self.ctx + (step + 8)) % 8

    def partner(self):
        return self.ctx + 1 - 2 * (self.ctx % 2)


def greet(here, plane=False, column=False, partner=False):
    barrier = pltpu.get_barrier_semaphore()
    who = []
    if plane:
        who += [(here.at(*step), here.ctx) for step in NEAR]
    if column:
        who += [(here.dp, here.peer(step)) for step in range(1, 8)]
    if partner:
        who += [(here.dp, here.partner())]
    for device in who:
        pl.semaphore_signal(barrier, inc=1, device_id=device, device_id_type=MESH)
    pl.semaphore_wait(barrier, len(who))


class Plane:
    SCRATCH = 7

    @staticmethod
    def scratch(rows, cols):
        return [pltpu.VMEM((14, rows // 2, cols), BF16), DMA((8,)), DMA((8,)), DMA((14,)), DMA((14,)), DMA((14,)), DMA((14,)), DMA]

    def __init__(self, here, send, recv, scratch):
        relay, near_s, near_r, first_s, first_r, last_s, last_r, own = scratch
        half = send.shape[1] // 2
        me = here.dp
        self.near, self.near_in, self.first, self.first_in, self.last, self.last_in = [], [], [], [], [], []
        self.own = pltpu.make_async_copy(send.at[me], recv.at[me], own)

        def remote(src, dst, s, r, device):
            return pltpu.make_async_remote_copy(
                src_ref=src, dst_ref=dst, send_sem=s, recv_sem=r, device_id=(device, here.ctx), device_id_type=MESH
            )

        for i, (dx, dy) in enumerate(NEAR):
            to, source = here.at(dx, dy), here.at(-dx, -dy)
            self.near.append(remote(send.at[to], recv.at[me], near_s.at[i], near_r.at[i], to))
            self.near_in.append(remote(recv.at[source], recv.at[source], near_s.at[i], near_r.at[i], to))
        for i, (dx, dy) in enumerate(FAR):
            for e in range(2):
                sign, n = 1 - 2 * e, 2 * i + e
                rows = pl.ds(e * half, half)
                one = (sign if dx == 2 else dx, sign if dy == 2 else dy)
                two = (sign if dx == 2 else 0, sign if dy == 2 else 0)
                via, final = here.at(*one), here.at(*two)
                origin, source = here.at(-one[0], -one[1]), here.at(-dx, -dy)
                slot = relay.at[n]
                self.first.append(remote(send.at[here.at(dx, dy), rows], slot, first_s.at[n], first_r.at[n], via))
                self.first_in.append(remote(slot, slot, first_s.at[n], first_r.at[n], via))
                self.last.append(remote(slot, recv.at[origin, rows], last_s.at[n], last_r.at[n], final))
                landing = recv.at[source, rows]
                self.last_in.append(remote(landing, landing, last_s.at[n], last_r.at[n], final))

    def start(self):
        for c in self.first + self.near:
            c.start()
        self.own.start()

    def forward(self):
        for arrived, c in zip(self.first_in, self.last):
            arrived.wait_recv()
            c.start()

    def finish_in(self):
        for c in self.near_in + self.last_in:
            c.wait_recv()
        self.own.wait()

    def finish_out(self):
        for c in self.near + self.first + self.last:
            c.wait_send()


class Column:
    @staticmethod
    def scratch():
        return [DMA((8,)), DMA((8,)), DMA]

    def __init__(self, here, source, target, scratch):
        send_s, recv_s, own = scratch
        self.out, self.into = [], []
        self.own = pltpu.make_async_copy(source(here.ctx), target(here.ctx), own)
        for i in range(1, 8):
            to, origin = here.peer(i), here.peer(-i)

            def remote(src, dst):
                return pltpu.make_async_remote_copy(
                    src_ref=src, dst_ref=dst, send_sem=send_s.at[i], recv_sem=recv_s.at[i],
                    device_id=(here.dp, to), device_id_type=MESH,
                )

            self.out.append(remote(source(to), target(here.ctx)))
            self.into.append(remote(target(origin), target(origin)))

    def start(self):
        for c in self.out:
            c.start()
        self.own.start()

    def finish_in(self):
        for c in self.into:
            c.wait_recv()
        self.own.wait()

    def finish_out(self):
        for c in self.out:
            c.wait_send()


def cols(start, width):
    return pl.ds(pl.multiple_of(start, 128), width)


def hot_of(place_ref, pair):
    return jnp.where(place_ref[pair : pair + 1] == (iota((384, 768), 0) + 1).astype(F32), 1.0, 0.0).astype(BF16)


def pack_pair(hots, z_ref, pair, out_ref):
    width = z_ref.shape[2]
    x = dot(hots[2 * pair], z_ref[2 * pair]) + dot(hots[2 * pair + 1], z_ref[2 * pair + 1])
    out_ref[:, 48 * pair : 48 * pair + 48] = x.astype(BF16).reshape(16, 48, width)


def in_kernel(row_ref, col_ref, k_ref, v_ref, q_ref, d_ref,
              slots_ref, place_ref, kv_ref, kt_ref, vt_ref, gq0_ref, gq1_ref, pd_ref,
              info, infos, kvs, zkv, zq0, zq1, zd, hots, skv, rkv, sq0, sq1, swap_s, swap_r, *sems):
    here = Here()
    parity = here.ctx % 2
    dest_r, dest_c = row_ref[...], col_ref[...]
    g_r, g_c = group_of(dest_r), group_of(dest_c)
    same = (g_r == g_c) & (iota((TOK, TOK), 0) < iota((TOK, TOK), 1))
    rank = jnp.sum(jnp.where(same, 1.0, 0.0), axis=0, keepdims=True).astype(jnp.int32) + CAP * parity
    which = iota((8, TOK), 0)
    info[...] = jnp.where(
        which == 0, g_r * 48 + rank, jnp.where(which == 1, place_of(dest_r) + 1, jnp.where(which == 2, g_r, rank))
    )
    for z in range(4):
        kvs[:, 2 * z * D : 2 * z * D + D] = k_ref[:, z * D : z * D + D]
        kvs[:, 2 * z * D + D : 2 * z * D + 2 * D] = v_ref[:, z * D : z * D + D]

    cs = [sems[3 * i : 3 * i + 3] for i in range(5)]
    ps = [sems[15 + 8 * i : 23 + 8 * i] for i in range(3)]
    a_info = Column(here, lambda p: info, lambda p: infos.at[p], cs[0])
    a_kv = Column(here, lambda p: kvs.at[:, cols(p * D, D)], lambda p: zkv.at[p], cs[1])
    a_q0 = Column(here, lambda p: q_ref.at[:, cols(p * 512, 256)], lambda p: zq0.at[p], cs[2])
    a_q1 = Column(here, lambda p: q_ref.at[:, cols(p * 512 + 256, 256)], lambda p: zq1.at[p], cs[3])
    a_d = Column(here, lambda p: d_ref.at[:, cols(p * 512, 512)], lambda p: zd.at[p], cs[4])
    b_kv = Plane(here, skv, rkv, ps[0])
    b_q0 = Plane(here, sq0, gq0_ref, ps[1])
    b_q1 = Plane(here, sq1, gq1_ref, ps[2])

    greet(here, plane=True, column=True)
    a_info.start()
    a_kv.start()
    a_q0.start()
    a_q1.start()
    a_info.finish_in()
    which = iota((16, 32, D), 1)
    tail = jnp.zeros((16, 32, D), F32)
    for pair in range(4):
        laid = jnp.zeros((16, D), F32)
        for c in (2 * pair, 2 * pair + 1):
            hots[c] = jnp.where(iota((768, TOK), 0) == infos[c, 0:1], 1.0, 0.0).astype(BF16)
            slots_ref[c : c + 1] = infos[c, 0:1].astype(F32)
            named = jnp.where(iota((16, TOK), 0) == infos[c, 2:3], infos[c, 1:2].astype(F32), 0.0).astype(BF16)
            laned = jnp.where(iota((D, TOK), 0) == infos[c, 3:4], 1.0, 0.0).astype(BF16)
            laid += dot(named, laned, NT)
        tail = jnp.where(which == pair, laid.reshape(16, 1, D), tail)
    a_kv.finish_in()
    for pair in range(4):
        pack_pair(hots, zkv, pair, skv)
    skv[:, TOK:] = tail.astype(BF16)
    b_kv.start()
    a_q0.finish_in()
    for pair in range(4):
        pack_pair(hots, zq0, pair, sq0)
    b_q0.start()
    b_kv.forward()
    a_q1.finish_in()
    a_d.start()
    for pair in range(4):
        pack_pair(hots, zq1, pair, sq1)
    b_q1.start()
    b_q0.forward()

    b_kv.finish_in()
    total = jnp.zeros((8, 768), F32)
    for s in range(16):
        mine = jnp.concatenate([rkv[s, TOK : TOK + 16].astype(F32)[:8], jnp.zeros((8, 640), F32)], axis=1)
        total += mine if s == 0 else pltpu.roll(mine, 48 * s, 1)
    odd = (iota((8, 768), 1) % 48) >= CAP
    place_ref[...] = jnp.where(odd & (total > 0.0), total + 192.0, total)
    for pair in range(4):
        x = rkv[:, 48 * pair : 48 * pair + 48].reshape(768, D)
        kv_ref[parity, 384 * pair : 384 * pair + 384] = dot(hot_of(place_ref, pair), x).astype(BF16)
    swap = pltpu.make_async_remote_copy(
        src_ref=kv_ref.at[parity], dst_ref=kv_ref.at[parity], send_sem=swap_s, recv_sem=swap_r,
        device_id=(here.dp, here.partner()), device_id_type=MESH,
    )
    swap.start()
    b_q1.forward()
    swapped = kv_ref.at[1 - parity]
    pltpu.make_async_remote_copy(
        src_ref=swapped, dst_ref=swapped, send_sem=swap_s, recv_sem=swap_r,
        device_id=(here.dp, here.partner()), device_id_type=MESH,
    ).wait_recv()
    kt_ref[...] = jnp.transpose(kv_ref[0].astype(F32)).astype(BF16)
    vt_ref[...] = jnp.transpose(kv_ref[1].astype(F32)).astype(BF16)
    a_d.finish_in()
    for pair in range(4):
        pack_pair(hots, zd, pair, pd_ref)
    b_q0.finish_in()
    b_q1.finish_in()
    swap.wait_send()
    for c in (a_info, a_kv, a_q0, a_q1, a_d, b_kv, b_q0, b_q1):
        c.finish_out()


def bring_in(destination, keys, values, queries, grad_out):
    return pl.pallas_call(
        in_kernel,
        out_shape=(
            jax.ShapeDtypeStruct((8, TOK), F32),
            jax.ShapeDtypeStruct((8, 768), F32),
            jax.ShapeDtypeStruct((2, 1536, D), BF16),
            jax.ShapeDtypeStruct((D, 1536), BF16),
            jax.ShapeDtypeStruct((D, 1536), BF16),
            jax.ShapeDtypeStruct((16, TOK, 256), BF16),
            jax.ShapeDtypeStruct((16, TOK, 256), BF16),
            jax.ShapeDtypeStruct((16, TOK, 512), BF16),
        ),
        in_specs=[VMEM] * 4 + [ANY] * 2,
        out_specs=(VMEM,) * 5 + (ANY, ANY, VMEM),
        scratch_shapes=[
            pltpu.VMEM((8, TOK), jnp.int32),
            pltpu.VMEM((8, 8, TOK), jnp.int32),
            pltpu.VMEM((TOK, 1024), BF16),
            pltpu.VMEM((8, TOK, D), BF16),
            pltpu.VMEM((8, TOK, 256), BF16),
            pltpu.VMEM((8, TOK, 256), BF16),
            pltpu.VMEM((8, TOK, 512), BF16),
            pltpu.VMEM((8, 768, TOK), BF16),
            pltpu.VMEM((16, TOK + 32, D), BF16),
            pltpu.VMEM((16, TOK + 32, D), BF16),
            pltpu.VMEM((16, TOK, 256), BF16),
            pltpu.VMEM((16, TOK, 256), BF16),
            DMA,
            DMA,
        ]
        + Column.scratch() * 5
        + Plane.scratch(TOK + 32, D) + Plane.scratch(TOK, 256) + Plane.scratch(TOK, 256),
        compiler_params=pltpu.CompilerParams(collective_id=0, has_side_effects=True, vmem_limit_bytes=44 << 20),
        name="bring_in",
    )(destination.reshape(1, TOK), destination.reshape(TOK, 1), keys, values, queries, grad_out)


def tiles():
    for j in range(6):
        low = 0 if j < 4 else 512
        yield j, list(range(low, (j + 1) * TILE, TILE))


def allowed(j, k, end):
    diagonal, mixed = k == j * TILE, j >= 2
    if not diagonal and not mixed:
        return None
    kp = k + iota((TILE, TILE), 0)
    qp = j * TILE + iota((1, TILE), 1)
    mask = None
    if mixed:
        mask = kp >= jnp.where(qp >= end, end, 0)
    if diagonal:
        causal = kp <= qp
        mask = causal if mask is None else mask & causal
    return mask


def forward_head(h, end, q_ref, k_ref, vt_ref, o_ref, lse_ref):
    for j, ks in tiles():
        rows = slice(j * TILE, j * TILE + TILE)
        q = q_ref[h, rows]
        scores = []
        for k in ks:
            s = dot(k_ref[0, k : k + TILE], q, NT)
            mask = allowed(j, k, end)
            scores.append(s if mask is None else jnp.where(mask, s, -jnp.inf))
        top = jnp.max(functools.reduce(jnp.maximum, scores), axis=0, keepdims=True)
        expo = [jnp.exp2((s - top) * EXP2) for s in scores]
        total = jnp.sum(functools.reduce(jnp.add, expo), axis=0, keepdims=True)
        inverse = 1.0 / total
        att = jnp.zeros((D, TILE), F32)
        for k, e in zip(ks, expo):
            att += dot(vt_ref[:, k : k + TILE], (e * inverse).astype(BF16))
        o_ref[h, rows] = jnp.transpose(att).astype(BF16)
        lse_ref[h, :, rows] = top * EXP2 + jnp.log2(total)


def forward_kernel(end_ref, place_ref, kv_ref, vt_ref, gq0_ref, gq1_ref, pd_ref,
                   q_ref, o_ref, lse_ref, po_ref, gd_ref, *sems):
    here = Here()
    b_d = Plane(here, pd_ref, gd_ref, sems)
    greet(here, plane=True)
    b_d.start()
    end = end_ref[0]
    for pair in range(4):
        hot = hot_of(place_ref, pair)
        for n, got in enumerate((gq0_ref, gq1_ref)):
            x = dot(hot, got[:, 48 * pair : 48 * pair + 48].reshape(768, 256)).astype(BF16)
            for h in range(2):
                q_ref[2 * n + h, 384 * pair : 384 * pair + 384] = x[:, h * D : h * D + D]

    @pl.loop(0, 2)
    def _(h):
        forward_head(h, end, q_ref, kv_ref, vt_ref, o_ref, lse_ref)

    b_d.forward()

    @pl.loop(2, 4)
    def _(h):
        forward_head(h, end, q_ref, kv_ref, vt_ref, o_ref, lse_ref)

    for pair in range(4):
        x = jnp.concatenate([o_ref[h, 384 * pair : 384 * pair + 384] for h in range(4)], axis=1)
        po_ref[:, 48 * pair : 48 * pair + 48] = dot(hot_of(place_ref, pair), x, TN).astype(BF16).reshape(16, 48, 512)
    b_d.finish_in()
    b_d.finish_out()


def forward(end, place, kv, vt, gq0, gq1, pd):
    return pl.pallas_call(
        forward_kernel,
        out_shape=(
            jax.ShapeDtypeStruct((4, 1536, D), BF16),
            jax.ShapeDtypeStruct((4, 1536, D), BF16),
            jax.ShapeDtypeStruct((4, 1, 1536), F32),
            jax.ShapeDtypeStruct((16, TOK, 512), BF16),
            jax.ShapeDtypeStruct((16, TOK, 512), BF16),
        ),
        in_specs=[SMEM] + [VMEM] * 5 + [ANY],
        out_specs=(VMEM,) * 4 + (ANY,),
        scratch_shapes=Plane.scratch(TOK, 512),
        compiler_params=pltpu.CompilerParams(collective_id=1, has_side_effects=True, vmem_limit_bytes=44 << 20),
        name="forward",
    )(end, place, kv, vt, gq0, gq1, pd)


def backward_head(h, end, q_ref, d_ref, o_ref, lse_ref, kv_ref, kt_ref, g_ref, gq_ref):
    for j, ks in tiles():
        rows = slice(j * TILE, j * TILE + TILE)
        q, d = q_ref[h, rows], d_ref[h, rows]
        product = d.astype(F32) * o_ref[h, rows].astype(F32)
        delta = jnp.sum(jnp.transpose(product), axis=0, keepdims=True)
        lse = lse_ref[h, :, rows]
        gq = jnp.zeros((D, TILE), F32)
        for k in ks:
            keys = slice(k, k + TILE)
            p = jnp.exp2(dot(kv_ref[0, keys], q, NT) * EXP2 - lse)
            mask = allowed(j, k, end)
            if mask is not None:
                p = jnp.where(mask, p, 0.0)
            dp = dot(kv_ref[1, keys], d, NT)
            ds = (p * (dp - delta)).astype(BF16)
            g_ref[1, keys] += dot(p.astype(BF16), d)
            g_ref[0, keys] += dot(ds, q)
            gq += dot(kt_ref[:, keys], ds)
        gq_ref[h, rows] = jnp.transpose(gq * SCALE).astype(BF16)


def backward_kernel(end_ref, place_ref, kv_ref, kt_ref, gd_ref, q_ref, o_ref, lse_ref, po_ref,
                    pq_ref, pkv_ref, go_ref,
                    d_ref, gq_ref, g_ref, landed, swap_s, swap_r, *sems):
    here = Here()
    parity = here.ctx % 2
    b_o = Plane(here, po_ref, go_ref, sems)
    greet(here, plane=True, partner=True)
    b_o.start()
    end = end_ref[0]
    g_ref[...] = jnp.zeros_like(g_ref)
    for pair in range(4):
        x = dot(hot_of(place_ref, pair), gd_ref[:, 48 * pair : 48 * pair + 48].reshape(768, 512)).astype(BF16)
        for h in range(4):
            d_ref[h, 384 * pair : 384 * pair + 384] = x[:, h * D : h * D + D]

    @pl.loop(0, 2)
    def _(h):
        backward_head(h, end, q_ref, d_ref, o_ref, lse_ref, kv_ref, kt_ref, g_ref, gq_ref)

    b_o.forward()

    @pl.loop(2, 4)
    def _(h):
        backward_head(h, end, q_ref, d_ref, o_ref, lse_ref, kv_ref, kt_ref, g_ref, gq_ref)

    swap = pltpu.make_async_remote_copy(
        src_ref=g_ref.at[1 - parity], dst_ref=landed, send_sem=swap_s, recv_sem=swap_r,
        device_id=(here.dp, here.partner()), device_id_type=MESH,
    )
    swap.start()
    for pair in range(4):
        x = jnp.concatenate([gq_ref[h, 384 * pair : 384 * pair + 384] for h in range(4)], axis=1)
        pq_ref[:, 48 * pair : 48 * pair + 48] = dot(hot_of(place_ref, pair), x, TN).astype(BF16).reshape(16, 48, 512)
    swap.wait_recv()
    factor = jnp.where(parity == 0, SCALE, 1.0).astype(F32)
    for pair in range(4):
        rows = slice(384 * pair, 384 * pair + 384)
        x = ((g_ref[parity, rows] + landed[rows]) * factor).astype(BF16)
        pkv_ref[:, 48 * pair : 48 * pair + 48] = dot(hot_of(place_ref, pair), x, TN).astype(BF16).reshape(16, 48, D)
    b_o.finish_in()
    swap.wait_send()
    b_o.finish_out()


def backward(end, place, kv, kt, gd, q, o, lse, po):
    return pl.pallas_call(
        backward_kernel,
        out_shape=(
            jax.ShapeDtypeStruct((16, TOK, 512), BF16),
            jax.ShapeDtypeStruct((16, TOK, D), BF16),
            jax.ShapeDtypeStruct((16, TOK, 512), BF16),
        ),
        in_specs=[SMEM] + [VMEM] * 7 + [ANY],
        out_specs=(VMEM, VMEM, ANY),
        scratch_shapes=[
            pltpu.VMEM((4, 1536, D), BF16),
            pltpu.VMEM((4, 1536, D), BF16),
            pltpu.VMEM((2, 1536, D), F32),
            pltpu.VMEM((1536, D), F32),
            DMA,
            DMA,
        ]
        + Plane.scratch(TOK, 512),
        compiler_params=pltpu.CompilerParams(collective_id=2, has_side_effects=True, vmem_limit_bytes=44 << 20),
        name="backward",
    )(end, place, kv, kt, gd, q, o, lse, po)


def out_kernel(slots_ref, go_ref, pq_ref, pkv_ref, oo_ref, oq_ref, ok_ref, ov_ref,
               gq, gkv, zo, zq, zkv, okv, hots, *sems):
    here = Here()
    cs = [sems[3 * i : 3 * i + 3] for i in range(3)]
    ps = [sems[9 + 8 * i : 17 + 8 * i] for i in range(2)]
    b_q = Plane(here, pq_ref, gq, ps[0])
    b_kv = Plane(here, pkv_ref, gkv, ps[1])
    a_o = Column(here, lambda p: zo.at[p], lambda p: oo_ref.at[:, cols(p * 512, 512)], cs[0])
    a_q = Column(here, lambda p: zq.at[p], lambda p: oq_ref.at[:, cols(p * 512, 512)], cs[1])
    a_kv = Column(here, lambda p: zkv.at[p], lambda p: okv.at[:, cols(p * D, D)], cs[2])
    greet(here, plane=True, column=True)
    b_q.start()
    b_kv.start()
    slot_c = jnp.transpose(slots_ref[...])

    def unpack(got, z):
        for pair in range(4):
            x = got[:, 48 * pair : 48 * pair + 48].reshape(768, got.shape[2])
            for c in (2 * pair, 2 * pair + 1):
                z[c] = dot(hots[c], x).astype(BF16)

    for c in range(8):
        hots[c] = jnp.where(iota((TOK, 768), 1).astype(F32) == slot_c[:, c : c + 1], 1.0, 0.0).astype(BF16)
    unpack(go_ref, zo)
    a_o.start()
    b_q.forward()
    b_kv.forward()
    b_q.finish_in()
    unpack(gq, zq)
    a_q.start()
    b_kv.finish_in()
    unpack(gkv, zkv)
    a_kv.start()
    a_kv.finish_in()
    for z in range(4):
        ok_ref[:, z * D : z * D + D] = okv[:, 2 * z * D : 2 * z * D + D]
        ov_ref[:, z * D : z * D + D] = okv[:, 2 * z * D + D : 2 * z * D + 2 * D]
    a_o.finish_in()
    a_q.finish_in()
    for c in (b_q, b_kv, a_o, a_q, a_kv):
        c.finish_out()


def take_back(slots, go, pq, pkv):
    return pl.pallas_call(
        out_kernel,
        out_shape=(
            jax.ShapeDtypeStruct((TOK, 4096), BF16),
            jax.ShapeDtypeStruct((TOK, 4096), BF16),
            jax.ShapeDtypeStruct((TOK, 512), BF16),
            jax.ShapeDtypeStruct((TOK, 512), BF16),
        ),
        in_specs=[VMEM, VMEM, ANY, ANY],
        out_specs=(ANY, ANY, VMEM, VMEM),
        scratch_shapes=[
            pltpu.VMEM((16, TOK, 512), BF16),
            pltpu.VMEM((16, TOK, D), BF16),
            pltpu.VMEM((8, TOK, 512), BF16),
            pltpu.VMEM((8, TOK, 512), BF16),
            pltpu.VMEM((8, TOK, D), BF16),
            pltpu.VMEM((TOK, 1024), BF16),
            pltpu.VMEM((8, TOK, 768), BF16),
        ]
        + Column.scratch() * 3
        + Plane.scratch(TOK, 512) + Plane.scratch(TOK, D),
        compiler_params=pltpu.CompilerParams(collective_id=3, has_side_effects=True, vmem_limit_bytes=44 << 20),
        name="take_back",
    )(slots, go, pq, pkv)


def local(queries, keys, values, grad_out, destination, lengths):
    end = lax.dynamic_slice(lengths, (lax.axis_index("dp"), 0), (1, 1)).reshape(1)
    slots, place, kv, kt, vt, gq0, gq1, pd = bring_in(destination, keys, values, queries, grad_out)
    q, o, lse, po, gd = forward(end, place, kv, vt, gq0, gq1, pd)
    pq, pkv, go = backward(end, place, kv, kt, gd, q, o, lse, po)
    return take_back(slots, go, pq, pkv)


def solution(mesh):
    rows = P(("dp", "ctx"), None)
    return jax.shard_map(
        local,
        mesh=mesh,
        in_specs=(rows, rows, rows, rows, P(("dp", "ctx")), P()),
        out_specs=(rows, rows, rows, rows),
        check_vma=False,
    )
```

```python
import functools
import math

import jax
import jax.numpy as jnp
from jax import lax
from jax.experimental import pallas as pl
from jax.experimental.pallas import tpu as pltpu
from jax.sharding import PartitionSpec as P

D = 128
TOK = 192
CAP = 24
F32 = jnp.float32
BF16 = jnp.bfloat16
MESH = pl.DeviceIdType.MESH
VMEM = pl.BlockSpec(memory_space=pltpu.VMEM)
SMEM = pl.BlockSpec(memory_space=pltpu.SMEM)
ANY = pl.BlockSpec(memory_space=pl.ANY)
HBM = pl.BlockSpec(memory_space=pltpu.HBM)
DMA = pltpu.SemaphoreType.DMA
NN = (((1,), (0,)), ((), ()))
NT = (((1,), (1,)), ((), ()))
TN = (((0,), (0,)), ((), ()))
TILE = 256
SCALE = 1.0 / math.sqrt(D)
EXP2 = SCALE * math.log2(math.e)


def dot(a, b, dims=NN):
    return lax.dot_general(a, b, dims, preferred_element_type=F32)


def iota(shape, axis):
    return lax.broadcasted_iota(jnp.int32, shape, axis)


def group_of(dest):
    return ((dest >> 9) * 43) >> 7


def place_of(dest):
    return dest - 192 * (((dest >> 6) * 171) >> 9)


STEPS = [(2, 2), (2, 1), (1, 2), (2, -1), (-1, 2), (1, 1), (-1, -1), (1, -1), (-1, 1), (2, 0), (0, 2),
         (1, 0), (-1, 0), (0, 1), (0, -1)]


class Here:
    def __init__(self):
        self.dp = lax.axis_index("dp")
        self.ctx = lax.axis_index("ctx")
        self.x, self.y = self.dp // 4, self.dp % 4

    def at(self, dx, dy):
        return ((self.x + (dx + 4)) % 4) * 4 + (self.y + (dy + 4)) % 4

    def peer(self, step):
        return (self.ctx + (step + 8)) % 8

    def partner(self):
        return self.ctx + 1 - 2 * (self.ctx % 2)


def greet(here, plane=False, column=False, partner=False):
    barrier = pltpu.get_barrier_semaphore()
    who = []
    if plane:
        who += [(here.at(*step), here.ctx) for step in STEPS]
    if column:
        who += [(here.dp, here.peer(step)) for step in range(1, 8)]
    if partner:
        who += [(here.dp, here.partner())]
    for device in who:
        pl.semaphore_signal(barrier, inc=1, device_id=device, device_id_type=MESH)
    pl.semaphore_wait(barrier, len(who))


class Plane:
    COUNT = 3

    @staticmethod
    def scratch():
        return [DMA((15,)), DMA((15,)), DMA]

    def __init__(self, here, send, recv, scratch, order=tuple(range(15))):
        send_s, recv_s, own = scratch
        me = here.dp
        self.out, self.into = [], []
        self.own = pltpu.make_async_copy(send.at[me], recv.at[me], own)
        for i in order:
            dx, dy = STEPS[i]
            to, source = here.at(dx, dy), here.at(-dx, -dy)

            def remote(src, dst):
                return pltpu.make_async_remote_copy(
                    src_ref=src, dst_ref=dst, send_sem=send_s.at[i], recv_sem=recv_s.at[i],
                    device_id=(to, here.ctx), device_id_type=MESH,
                )

            self.out.append(remote(send.at[to], recv.at[me]))
            self.into.append(remote(recv.at[source], recv.at[source]))

    def start(self):
        for c in self.out:
            c.start()
        self.own.start()

    def finish_in(self):
        for c in self.into:
            c.wait_recv()
        self.own.wait()

    def finish_out(self):
        for c in self.out:
            c.wait_send()


class Column:
    @staticmethod
    def scratch():
        return [DMA((8,)), DMA((8,)), DMA]

    def __init__(self, here, source, target, scratch):
        send_s, recv_s, own = scratch
        self.out, self.into = [], []
        self.own = pltpu.make_async_copy(source(here.ctx), target(here.ctx), own)
        for i in range(1, 8):
            to, origin = here.peer(i), here.peer(-i)

            def remote(src, dst):
                return pltpu.make_async_remote_copy(
                    src_ref=src, dst_ref=dst, send_sem=send_s.at[i], recv_sem=recv_s.at[i],
                    device_id=(here.dp, to), device_id_type=MESH,
                )

            self.out.append(remote(source(to), target(here.ctx)))
            self.into.append(remote(target(origin), target(origin)))

    def start(self):
        for c in self.out:
            c.start()
        self.own.start()

    def finish_in(self):
        for c in self.into:
            c.wait_recv()
        self.own.wait()

    def finish_out(self):
        for c in self.out:
            c.wait_send()


def cols(start, width):
    return pl.ds(pl.multiple_of(start, 128), width)


def hot_of(place_ref, pair):
    return jnp.where(place_ref[pair : pair + 1] == (iota((384, 768), 0) + 1).astype(F32), 1.0, 0.0).astype(BF16)


def pack_pair(hots, z_ref, pair, out_ref):
    width = z_ref.shape[2]
    x = dot(hots[2 * pair], z_ref[2 * pair]) + dot(hots[2 * pair + 1], z_ref[2 * pair + 1])
    out_ref[:, 48 * pair : 48 * pair + 48] = x.astype(BF16).reshape(16, 48, width)


def in_kernel(row_ref, k_ref, v_ref, q_ref, d_ref,
              slots_ref, place_ref, kv_ref, kt_ref, vt_ref, gq0_ref, gq1_ref, pd_ref,
              load, info, infos, kvs, zkv, zq0, zq1, zd, hots, skv, rkv, sq0, sq1, swap_s, swap_r, *sems):
    here = Here()
    parity = here.ctx % 2
    loads = []
    for z in range(4):
        for e, ref in enumerate((k_ref, v_ref)):
            to = kvs.at[:, pl.ds((2 * z + e) * D, D)]
            loads.append(pltpu.make_async_copy(ref.at[:, pl.ds(z * D, D)], to, load.at[2 * z + e]))
    for c in loads:
        c.start()
    dest_r = row_ref[...]
    g_r = group_of(dest_r)
    g_c = jnp.transpose(jnp.broadcast_to(g_r.astype(F32), (8, TOK)))[:, 0:1]
    same = (g_r.astype(F32) == g_c) & (iota((TOK, TOK), 0) < iota((TOK, TOK), 1))
    rank = jnp.sum(jnp.where(same, 1.0, 0.0), axis=0, keepdims=True).astype(jnp.int32) + CAP * parity
    which = iota((8, TOK), 0)
    info[...] = jnp.where(
        which == 0, g_r * 48 + rank, jnp.where(which == 1, place_of(dest_r) + 1, jnp.where(which == 2, g_r, rank))
    )
    for c in loads:
        c.wait()
    cs = [sems[3 * i : 3 * i + 3] for i in range(5)]
    ps = [sems[15 + 3 * i : 18 + 3 * i] for i in range(3)]
    a_info = Column(here, lambda p: info, lambda p: infos.at[p], cs[0])
    a_kv = Column(here, lambda p: kvs.at[:, cols(p * D, D)], lambda p: zkv.at[p], cs[1])
    a_q0 = Column(here, lambda p: q_ref.at[:, cols(p * 512, 256)], lambda p: zq0.at[p], cs[2])
    a_q1 = Column(here, lambda p: q_ref.at[:, cols(p * 512 + 256, 256)], lambda p: zq1.at[p], cs[3])
    a_d = Column(here, lambda p: d_ref.at[:, cols(p * 512, 512)], lambda p: zd.at[p], cs[4])
    b_kv = Plane(here, skv, rkv, ps[0])
    b_q0 = Plane(here, sq0, gq0_ref, ps[1])
    b_q1 = Plane(here, sq1, gq1_ref, ps[2])

    greet(here, plane=True, column=True)
    a_info.start()
    a_kv.start()
    a_q0.start()
    a_q1.start()
    a_info.finish_in()
    which = iota((16, 32, D), 1)
    tail = jnp.zeros((16, 32, D), F32)
    for pair in range(4):
        laid = jnp.zeros((16, D), F32)
        for c in (2 * pair, 2 * pair + 1):
            hots[c] = jnp.where(iota((768, TOK), 0) == infos[c, 0:1], 1.0, 0.0).astype(BF16)
            slots_ref[c : c + 1] = infos[c, 0:1].astype(F32)
            named = jnp.where(iota((16, TOK), 0) == infos[c, 2:3], infos[c, 1:2].astype(F32), 0.0).astype(BF16)
            laned = jnp.where(iota((D, TOK), 0) == infos[c, 3:4], 1.0, 0.0).astype(BF16)
            laid += dot(named, laned, NT)
        tail = jnp.where(which == pair, laid.reshape(16, 1, D), tail)
    a_kv.finish_in()
    for pair in range(4):
        pack_pair(hots, zkv, pair, skv)
    skv[:, TOK:] = tail.astype(BF16)
    b_kv.start()
    a_q0.finish_in()
    for pair in range(4):
        pack_pair(hots, zq0, pair, sq0)
    b_q0.start()
    a_q1.finish_in()
    a_d.start()
    for pair in range(4):
        pack_pair(hots, zq1, pair, sq1)
    b_q1.start()

    b_kv.finish_in()
    total = jnp.zeros((8, 768), F32)
    for s in range(16):
        mine = jnp.concatenate([rkv[s, TOK : TOK + 16].astype(F32)[:8], jnp.zeros((8, 640), F32)], axis=1)
        total += mine if s == 0 else pltpu.roll(mine, 48 * s, 1)
    odd = (iota((8, 768), 1) % 48) >= CAP
    place_ref[...] = jnp.where(odd & (total > 0.0), total + 192.0, total)
    for pair in range(4):
        x = rkv[:, 48 * pair : 48 * pair + 48].reshape(768, D)
        kv_ref[parity, 384 * pair : 384 * pair + 384] = dot(hot_of(place_ref, pair), x).astype(BF16)
    swap = pltpu.make_async_remote_copy(
        src_ref=kv_ref.at[parity], dst_ref=kv_ref.at[parity], send_sem=swap_s, recv_sem=swap_r,
        device_id=(here.dp, here.partner()), device_id_type=MESH,
    )
    swap.start()
    swapped = kv_ref.at[1 - parity]
    pltpu.make_async_remote_copy(
        src_ref=swapped, dst_ref=swapped, send_sem=swap_s, recv_sem=swap_r,
        device_id=(here.dp, here.partner()), device_id_type=MESH,
    ).wait_recv()
    kt_ref[...] = jnp.transpose(kv_ref[0].astype(F32)).astype(BF16)
    vt_ref[...] = jnp.transpose(kv_ref[1].astype(F32)).astype(BF16)
    a_d.finish_in()
    for pair in range(4):
        pack_pair(hots, zd, pair, pd_ref)
    b_q0.finish_in()
    b_q1.finish_in()
    swap.wait_send()
    for c in (a_info, a_kv, a_q0, a_q1, a_d, b_kv, b_q0, b_q1):
        c.finish_out()


def bring_in(destination, keys, values, queries, grad_out):
    return pl.pallas_call(
        in_kernel,
        out_shape=(
            jax.ShapeDtypeStruct((8, TOK), F32),
            jax.ShapeDtypeStruct((8, 768), F32),
            jax.ShapeDtypeStruct((2, 1536, D), BF16),
            jax.ShapeDtypeStruct((D, 1536), BF16),
            jax.ShapeDtypeStruct((D, 1536), BF16),
            jax.ShapeDtypeStruct((16, TOK, 256), BF16),
            jax.ShapeDtypeStruct((16, TOK, 256), BF16),
            jax.ShapeDtypeStruct((16, TOK, 512), BF16),
        ),
        in_specs=[VMEM] + [HBM] * 4,
        out_specs=(VMEM,) * 5 + (ANY, ANY, VMEM),
        scratch_shapes=[
            DMA((8,)),
            pltpu.VMEM((8, TOK), jnp.int32),
            pltpu.VMEM((8, 8, TOK), jnp.int32),
            pltpu.VMEM((TOK, 1024), BF16),
            pltpu.VMEM((8, TOK, D), BF16),
            pltpu.VMEM((8, TOK, 256), BF16),
            pltpu.VMEM((8, TOK, 256), BF16),
            pltpu.VMEM((8, TOK, 512), BF16),
            pltpu.VMEM((8, 768, TOK), BF16),
            pltpu.VMEM((16, TOK + 32, D), BF16),
            pltpu.VMEM((16, TOK + 32, D), BF16),
            pltpu.VMEM((16, TOK, 256), BF16),
            pltpu.VMEM((16, TOK, 256), BF16),
            DMA,
            DMA,
        ]
        + Column.scratch() * 5
        + Plane.scratch() * 3,
        compiler_params=pltpu.CompilerParams(collective_id=0, has_side_effects=True, vmem_limit_bytes=44 << 20),
        name="bring_in",
    )(destination.reshape(1, TOK), keys, values, queries, grad_out)


def tiles():
    for j in range(6):
        low = 0 if j < 4 else 512
        yield j, list(range(low, (j + 1) * TILE, TILE))


def allowed(j, k, end):
    diagonal, mixed = k == j * TILE, j >= 2
    if not diagonal and not mixed:
        return None
    kp = k + iota((TILE, TILE), 0)
    qp = j * TILE + iota((1, TILE), 1)
    mask = None
    if mixed:
        mask = kp >= jnp.where(qp >= end, end, 0)
    if diagonal:
        causal = kp <= qp
        mask = causal if mask is None else mask & causal
    return mask


def forward_head(h, end, q_ref, k_ref, vt_ref, o_ref, lse_ref):
    for j, ks in tiles():
        rows = slice(j * TILE, j * TILE + TILE)
        q = q_ref[h, rows]
        scores = []
        for k in ks:
            s = dot(k_ref[0, k : k + TILE], q, NT)
            mask = allowed(j, k, end)
            scores.append(s if mask is None else jnp.where(mask, s, -jnp.inf))
        top = jnp.max(functools.reduce(jnp.maximum, scores), axis=0, keepdims=True)
        expo = [jnp.exp2((s - top) * EXP2) for s in scores]
        total = jnp.sum(functools.reduce(jnp.add, expo), axis=0, keepdims=True)
        inverse = 1.0 / total
        att = jnp.zeros((D, TILE), F32)
        for k, e in zip(ks, expo):
            att += dot(vt_ref[:, k : k + TILE], (e * inverse).astype(BF16))
        o_ref[h, rows] = jnp.transpose(att).astype(BF16)
        lse_ref[h, :, rows] = top * EXP2 + jnp.log2(total)


def forward_kernel(end_ref, place_ref, kv_ref, vt_ref, gq0_ref, gq1_ref, pd_ref,
                   q_ref, o_ref, lse_ref, po_ref, gd_ref, *sems):
    here = Here()
    b_d = Plane(here, pd_ref, gd_ref, sems)
    greet(here, plane=True)
    b_d.start()
    end = end_ref[here.dp, 0]
    for pair in range(4):
        hot = hot_of(place_ref, pair)
        for n, got in enumerate((gq0_ref, gq1_ref)):
            x = dot(hot, got[:, 48 * pair : 48 * pair + 48].reshape(768, 256)).astype(BF16)
            for h in range(2):
                q_ref[2 * n + h, 384 * pair : 384 * pair + 384] = x[:, h * D : h * D + D]

    @pl.loop(0, 2)
    def _(h):
        forward_head(h, end, q_ref, kv_ref, vt_ref, o_ref, lse_ref)


    @pl.loop(2, 4)
    def _(h):
        forward_head(h, end, q_ref, kv_ref, vt_ref, o_ref, lse_ref)

    for pair in range(4):
        x = jnp.concatenate([o_ref[h, 384 * pair : 384 * pair + 384] for h in range(4)], axis=1)
        po_ref[:, 48 * pair : 48 * pair + 48] = dot(hot_of(place_ref, pair), x, TN).astype(BF16).reshape(16, 48, 512)
    b_d.finish_in()
    b_d.finish_out()


def forward(lengths, place, kv, vt, gq0, gq1, pd):
    return pl.pallas_call(
        forward_kernel,
        out_shape=(
            jax.ShapeDtypeStruct((4, 1536, D), BF16),
            jax.ShapeDtypeStruct((4, 1536, D), BF16),
            jax.ShapeDtypeStruct((4, 1, 1536), F32),
            jax.ShapeDtypeStruct((16, TOK, 512), BF16),
            jax.ShapeDtypeStruct((16, TOK, 512), BF16),
        ),
        in_specs=[SMEM] + [VMEM] * 5 + [ANY],
        out_specs=(VMEM,) * 4 + (ANY,),
        scratch_shapes=Plane.scratch(),
        compiler_params=pltpu.CompilerParams(collective_id=1, has_side_effects=True, vmem_limit_bytes=44 << 20),
        name="forward",
    )(lengths, place, kv, vt, gq0, gq1, pd)


def backward_head(h, end, q_ref, d_ref, o_ref, lse_ref, kv_ref, kt_ref, g_ref, gq_ref):
    for j, ks in tiles():
        rows = slice(j * TILE, j * TILE + TILE)
        q, d = q_ref[h, rows], d_ref[h, rows]
        product = d.astype(F32) * o_ref[h, rows].astype(F32)
        delta = jnp.sum(jnp.transpose(product), axis=0, keepdims=True)
        lse = lse_ref[h, :, rows]
        gq = jnp.zeros((D, TILE), F32)
        for k in ks:
            keys = slice(k, k + TILE)
            p = jnp.exp2(dot(kv_ref[0, keys], q, NT) * EXP2 - lse)
            mask = allowed(j, k, end)
            if mask is not None:
                p = jnp.where(mask, p, 0.0)
            dp = dot(kv_ref[1, keys], d, NT)
            ds = (p * (dp - delta)).astype(BF16)
            g_ref[1, keys] += dot(p.astype(BF16), d)
            g_ref[0, keys] += dot(ds, q)
            gq += dot(kt_ref[:, keys], ds)
        gq_ref[h, rows] = jnp.transpose(gq * SCALE).astype(BF16)


def backward_kernel(end_ref, place_ref, kv_ref, kt_ref, gd_ref, q_ref, o_ref, lse_ref, po_ref,
                    pq0_ref, pq1_ref, pkv_ref, go_ref,
                    d_ref, gq_ref, g_ref, landed, swap_s, swap_r, *sems):
    here = Here()
    parity = here.ctx % 2
    b_o = Plane(here, po_ref, go_ref, sems, order=(11, 12, 13, 14, 9, 10, 5, 6, 7, 8, 1, 2, 3, 4, 0))
    greet(here, plane=True, partner=True)
    b_o.start()
    end = end_ref[here.dp, 0]
    g_ref[...] = jnp.zeros_like(g_ref)
    for pair in range(4):
        x = dot(hot_of(place_ref, pair), gd_ref[:, 48 * pair : 48 * pair + 48].reshape(768, 512)).astype(BF16)
        for h in range(4):
            d_ref[h, 384 * pair : 384 * pair + 384] = x[:, h * D : h * D + D]

    @pl.loop(0, 4)
    def _(h):
        backward_head(h, end, q_ref, d_ref, o_ref, lse_ref, kv_ref, kt_ref, g_ref, gq_ref)

    swap = pltpu.make_async_remote_copy(
        src_ref=g_ref.at[1 - parity], dst_ref=landed, send_sem=swap_s, recv_sem=swap_r,
        device_id=(here.dp, here.partner()), device_id_type=MESH,
    )
    swap.start()
    for pair in range(4):
        x = jnp.concatenate([gq_ref[h, 384 * pair : 384 * pair + 384] for h in range(4)], axis=1)
        packed = dot(hot_of(place_ref, pair), x, TN).astype(BF16).reshape(16, 48, 512)
        pq0_ref[:, 48 * pair : 48 * pair + 48] = packed[:, :, :256]
        pq1_ref[:, 48 * pair : 48 * pair + 48] = packed[:, :, 256:]
    swap.wait_recv()
    factor = jnp.where(parity == 0, SCALE, 1.0).astype(F32)
    for pair in range(4):
        rows = slice(384 * pair, 384 * pair + 384)
        x = ((g_ref[parity, rows] + landed[rows]) * factor).astype(BF16)
        pkv_ref[:, 48 * pair : 48 * pair + 48] = dot(hot_of(place_ref, pair), x, TN).astype(BF16).reshape(16, 48, D)
    b_o.finish_in()
    swap.wait_send()
    b_o.finish_out()


def backward(lengths, place, kv, kt, gd, q, o, lse, po):
    return pl.pallas_call(
        backward_kernel,
        out_shape=(
            jax.ShapeDtypeStruct((16, TOK, 256), BF16),
            jax.ShapeDtypeStruct((16, TOK, 256), BF16),
            jax.ShapeDtypeStruct((16, TOK, D), BF16),
            jax.ShapeDtypeStruct((16, TOK, 512), BF16),
        ),
        in_specs=[SMEM] + [VMEM] * 7 + [ANY],
        out_specs=(VMEM, VMEM, VMEM, ANY),
        scratch_shapes=[
            pltpu.VMEM((4, 1536, D), BF16),
            pltpu.VMEM((4, 1536, D), BF16),
            pltpu.VMEM((2, 1536, D), F32),
            pltpu.VMEM((1536, D), F32),
            DMA,
            DMA,
        ]
        + Plane.scratch(),
        compiler_params=pltpu.CompilerParams(collective_id=2, has_side_effects=True, vmem_limit_bytes=44 << 20),
        name="backward",
    )(lengths, place, kv, kt, gd, q, o, lse, po)


def out_kernel(slots_ref, go_ref, pq0_ref, pq1_ref, pkv_ref, oo_ref, oq_ref, ok_ref, ov_ref,
               gq0, gq1, gkv, zo, zq0, zq1, zkv, okv, hots, *sems):
    here = Here()
    cs = [sems[3 * i : 3 * i + 3] for i in range(4)]
    ps = [sems[12 + 3 * i : 15 + 3 * i] for i in range(3)]
    b_q0 = Plane(here, pq0_ref, gq0, ps[0])
    b_q1 = Plane(here, pq1_ref, gq1, ps[1])
    b_kv = Plane(here, pkv_ref, gkv, ps[2])
    a_o = Column(here, lambda p: zo.at[p], lambda p: oo_ref.at[:, cols(p * 512, 512)], cs[0])
    a_q0 = Column(here, lambda p: zq0.at[p], lambda p: oq_ref.at[:, cols(p * 512, 256)], cs[1])
    a_q1 = Column(here, lambda p: zq1.at[p], lambda p: oq_ref.at[:, cols(p * 512 + 256, 256)], cs[2])
    a_kv = Column(here, lambda p: zkv.at[p], lambda p: okv.at[:, cols(p * D, D)], cs[3])
    greet(here, plane=True, column=True)
    b_q0.start()
    b_q1.start()
    b_kv.start()
    slot_c = jnp.transpose(slots_ref[...])

    def unpack(got, z):
        for pair in range(4):
            x = got[:, 48 * pair : 48 * pair + 48].reshape(768, got.shape[2])
            for c in (2 * pair, 2 * pair + 1):
                z[c] = dot(hots[c], x).astype(BF16)

    for c in range(8):
        hots[c] = jnp.where(iota((TOK, 768), 1).astype(F32) == slot_c[:, c : c + 1], 1.0, 0.0).astype(BF16)
    unpack(go_ref, zo)
    a_o.start()
    b_q0.finish_in()
    unpack(gq0, zq0)
    a_q0.start()
    b_q1.finish_in()
    unpack(gq1, zq1)
    a_q1.start()
    b_kv.finish_in()
    unpack(gkv, zkv)
    a_kv.start()
    a_o.finish_in()
    a_q0.finish_in()
    a_q1.finish_in()
    a_kv.finish_in()
    for z in range(4):
        ok_ref[:, z * D : z * D + D] = okv[:, 2 * z * D : 2 * z * D + D]
        ov_ref[:, z * D : z * D + D] = okv[:, 2 * z * D + D : 2 * z * D + 2 * D]
    for c in (b_q0, b_q1, b_kv, a_o, a_q0, a_q1, a_kv):
        c.finish_out()


def take_back(slots, go, pq0, pq1, pkv):
    return pl.pallas_call(
        out_kernel,
        out_shape=(
            jax.ShapeDtypeStruct((TOK, 4096), BF16),
            jax.ShapeDtypeStruct((TOK, 4096), BF16),
            jax.ShapeDtypeStruct((TOK, 512), BF16),
            jax.ShapeDtypeStruct((TOK, 512), BF16),
        ),
        in_specs=[VMEM, VMEM, ANY, ANY, ANY],
        out_specs=(ANY, ANY, VMEM, VMEM),
        scratch_shapes=[
            pltpu.VMEM((16, TOK, 256), BF16),
            pltpu.VMEM((16, TOK, 256), BF16),
            pltpu.VMEM((16, TOK, D), BF16),
            pltpu.VMEM((8, TOK, 512), BF16),
            pltpu.VMEM((8, TOK, 256), BF16),
            pltpu.VMEM((8, TOK, 256), BF16),
            pltpu.VMEM((8, TOK, D), BF16),
            pltpu.VMEM((TOK, 1024), BF16),
            pltpu.VMEM((8, TOK, 768), BF16),
        ]
        + Column.scratch() * 4
        + Plane.scratch() * 3,
        compiler_params=pltpu.CompilerParams(collective_id=3, has_side_effects=True, vmem_limit_bytes=44 << 20),
        name="take_back",
    )(slots, go, pq0, pq1, pkv)


def local(queries, keys, values, grad_out, destination, lengths):
    slots, place, kv, kt, vt, gq0, gq1, pd = bring_in(destination, keys, values, queries, grad_out)
    q, o, lse, po, gd = forward(lengths, place, kv, vt, gq0, gq1, pd)
    pq0, pq1, pkv, go = backward(lengths, place, kv, kt, gd, q, o, lse, po)
    return take_back(slots, go, pq0, pq1, pkv)


def solution(mesh):
    rows = P(("dp", "ctx"), None)
    return jax.shard_map(
        local,
        mesh=mesh,
        in_specs=(rows, rows, rows, rows, P(("dp", "ctx")), P()),
        out_specs=(rows, rows, rows, rows),
        check_vma=False,
    )
```

```python
import functools
import math

import jax
import jax.numpy as jnp
from jax import lax
from jax.experimental import pallas as pl
from jax.experimental.pallas import tpu as pltpu
from jax.sharding import PartitionSpec as P

D = 128
TOK = 192
CAP = 24
F32 = jnp.float32
BF16 = jnp.bfloat16
MESH = pl.DeviceIdType.MESH
VMEM = pl.BlockSpec(memory_space=pltpu.VMEM)
SMEM = pl.BlockSpec(memory_space=pltpu.SMEM)
HBM = pl.BlockSpec(memory_space=pltpu.HBM)
DMA = pltpu.SemaphoreType.DMA
NN = (((1,), (0,)), ((), ()))
NT = (((1,), (1,)), ((), ()))
TN = (((0,), (0,)), ((), ()))
TILE = 256
SCALE = 1.0 / math.sqrt(D)
EXP2 = SCALE * math.log2(math.e)


def dot(a, b, dims=NN):
    return lax.dot_general(a, b, dims, preferred_element_type=F32)


def iota(shape, axis):
    return lax.broadcasted_iota(jnp.int32, shape, axis)


def group_of(dest):
    return ((dest >> 9) * 43) >> 7


def place_of(dest):
    return dest - 192 * (((dest >> 6) * 171) >> 9)


STEPS = [(1, 0), (-1, 0), (0, 1), (0, -1), (2, 0), (0, 2), (1, 1), (-1, -1), (1, -1), (-1, 1),
         (2, 1), (1, 2), (2, -1), (-1, 2), (2, 2)]
INWARD = (0, 3, 1, 2)
OUTWARD = (2, 1, 3, 0)


class Here:
    def __init__(self):
        self.dp = lax.axis_index("dp")
        self.ctx = lax.axis_index("ctx")
        self.x, self.y = self.dp // 4, self.dp % 4
        self.z, self.core = self.ctx // 2, self.ctx % 2

    def at(self, dx, dy):
        return ((self.x + (dx + 4)) % 4) * 4 + (self.y + (dy + 4)) % 4

    def chip(self, dz):
        return (self.z + (dz + 4)) % 4

    def peer(self, dz, other):
        return self.chip(dz) * 2 + (self.core + other) % 2


def greet(here):
    barrier = pltpu.get_barrier_semaphore()
    who = [(here.at(*step), here.ctx) for step in STEPS] + [(here.dp, here.peer(*step)) for step in COLUMN[1:]]
    for device in who:
        pl.semaphore_signal(barrier, inc=1, device_id=device, device_id_type=MESH)
    pl.semaphore_wait(barrier, len(who))


def remote(src, dst, send_sem, recv_sem, device):
    return pltpu.make_async_remote_copy(
        src_ref=src, dst_ref=dst, send_sem=send_sem, recv_sem=recv_sem, device_id=device, device_id_type=MESH
    )


class Plane:
    @staticmethod
    def scratch(parts):
        return [DMA((parts, 15)), DMA((parts, 15)), DMA((parts,))]

    def __init__(self, here, send, recv, scratch, rows):
        self.here, self.send, self.recv, self.rows = here, send, recv, rows
        self.send_s, self.recv_s, self.own_s = scratch
        self.begun = []

    def own(self, part):
        me, rows = self.here.dp, self.rows(part)
        return pltpu.make_async_copy(self.send.at[me, rows], self.recv.at[me, rows], self.own_s.at[part])

    def start(self, part=0):
        rows = self.rows(part)
        for i, (dx, dy) in enumerate(STEPS):
            to = self.here.at(dx, dy)
            c = remote(self.send.at[to, rows], self.recv.at[self.here.dp, rows],
                       self.send_s.at[part, i], self.recv_s.at[part, i], (to, self.here.ctx))
            c.start()
            self.begun.append(c)
        self.own(part).start()

    def finish_in(self, part=0):
        rows = self.rows(part)
        for i, (dx, dy) in enumerate(STEPS):
            source = self.here.at(-dx, -dy)
            landing = self.recv.at[source, rows]
            remote(landing, landing, self.send_s.at[part, i], self.recv_s.at[part, i], (source, self.here.ctx)).wait_recv()
        self.own(part).wait()

    def finish_out(self):
        for c in self.begun:
            c.wait_send()


COLUMN = [(0, 0), (0, 1), (1, 0), (1, 1), (3, 0), (3, 1), (2, 0), (2, 1)]


class Column:
    @staticmethod
    def scratch():
        return [DMA((8,)), DMA((8,)), DMA]

    def __init__(self, here, source, target, scratch):
        self.here, self.source, self.target = here, source, target
        self.send_s, self.recv_s, self.own_s = scratch
        self.own = pltpu.make_async_copy(source(here.ctx), target(here.ctx), self.own_s)
        self.begun = []

    def start_chip(self, dz):
        for other in range(2):
            if (dz, other) == (0, 0):
                self.own.start()
                continue
            to, n = self.here.peer(dz, other), 2 * dz + other
            c = remote(self.source(to), self.target(self.here.ctx), self.send_s.at[n], self.recv_s.at[n], (self.here.dp, to))
            c.start()
            self.begun.append(c)

    def start(self):
        for dz in (0, 1, 3, 2):
            self.start_chip(dz)

    def finish_chip(self, dz):
        for other in range(2):
            n = 2 * ((4 - dz) % 4) + other
            if n == 0:
                self.own.wait()
                continue
            origin = self.here.peer(dz, other)
            landing = self.target(origin)
            remote(landing, landing, self.send_s.at[n], self.recv_s.at[n], (self.here.dp, origin)).wait_recv()

    def finish_in(self):
        for dz in range(4):
            self.finish_chip(dz)

    def finish_out(self):
        for c in self.begun:
            c.wait_send()


def cols(start, width):
    return pl.ds(pl.multiple_of(start, 128), width)


def hot_of(place_ref, pair):
    return jnp.where(place_ref[pl.ds(pair, 1)] == (iota((384, 768), 0) + 1).astype(F32), 1.0, 0.0).astype(BF16)


def rows48(pair):
    return pl.ds(pl.multiple_of(48 * pair, 16), 48)


def rows384(pair):
    return pl.ds(pl.multiple_of(384 * pair, 128), 384)


def pack_pair(hots, z_ref, pair, out_ref):
    x = dot(hots[2 * pair], z_ref[2 * pair]) + dot(hots[2 * pair + 1], z_ref[2 * pair + 1])
    out_ref[:, rows48(pair)] = x.astype(BF16).reshape(16, 48, z_ref.shape[2])


def unpack_pair(backs, got, pair, z_ref):
    x = got[:, rows48(pair)].reshape(768, got.shape[2])
    for c in range(2):
        z_ref[2 * pair + c] = dot(backs[2 * pair + c], x).astype(BF16)


def regroup(place_ref, got, pair):
    return dot(hot_of(place_ref, pair), got[:, rows48(pair)].reshape(768, got.shape[2]))


def return_pair(place_ref, x, pair, out_ref):
    packed = dot(hot_of(place_ref, pair), x, TN).astype(BF16)
    out_ref[:, rows48(pair)] = packed.reshape(16, 48, x.shape[1])


def tiles():
    for j in range(6):
        low = 0 if j < 4 else 512
        yield j, list(range(low, (j + 1) * TILE, TILE))


def allowed(j, k, end):
    diagonal, mixed = k == j * TILE, j >= 2
    if not diagonal and not mixed:
        return None
    kp = k + iota((TILE, TILE), 0)
    qp = j * TILE + iota((1, TILE), 1)
    mask = None
    if mixed:
        mask = kp >= jnp.where(qp >= end, end, 0)
    if diagonal:
        causal = kp <= qp
        mask = causal if mask is None else mask & causal
    return mask


def forward_head(h, end, q_ref, kv_ref, vt_ref, o_ref, lse_ref):
    for j, ks in tiles():
        rows = slice(j * TILE, j * TILE + TILE)
        q = q_ref[h, rows]
        scores = []
        for k in ks:
            s = dot(kv_ref[0, k : k + TILE], q, NT)
            mask = allowed(j, k, end)
            scores.append(s if mask is None else jnp.where(mask, s, -jnp.inf))
        top = jnp.max(functools.reduce(jnp.maximum, scores), axis=0, keepdims=True)
        expo = [jnp.exp2((s - top) * EXP2) for s in scores]
        total = jnp.sum(functools.reduce(jnp.add, expo), axis=0, keepdims=True)
        inverse = 1.0 / total
        att = jnp.zeros((D, TILE), F32)
        for k, e in zip(ks, expo):
            att += dot(vt_ref[:, k : k + TILE], (e * inverse).astype(BF16))
        o_ref[h, rows] = jnp.transpose(att).astype(BF16)
        lse_ref[h, :, rows] = top * EXP2 + jnp.log2(total)


def backward_head(h, end, q_ref, d_ref, o_ref, lse_ref, kv_ref, kt_ref, g_ref, gq_ref):
    for j, ks in tiles():
        rows = slice(j * TILE, j * TILE + TILE)
        q, d = q_ref[h, rows], d_ref[h, rows]
        product = d.astype(F32) * o_ref[h, rows].astype(F32)
        delta = jnp.sum(jnp.transpose(product), axis=0, keepdims=True)
        lse = lse_ref[h, :, rows]
        gq = jnp.zeros((D, TILE), F32)
        for k in ks:
            keys = slice(k, k + TILE)
            p = jnp.exp2(dot(kv_ref[0, keys], q, NT) * EXP2 - lse)
            mask = allowed(j, k, end)
            if mask is not None:
                p = jnp.where(mask, p, 0.0)
            dp = dot(kv_ref[1, keys], d, NT)
            ds = (p * (dp - delta)).astype(BF16)
            g_ref[1, keys] += dot(p.astype(BF16), d)
            g_ref[0, keys] += dot(ds, q)
            gq += dot(kt_ref[:, keys], ds)
        gq_ref[h, rows] = jnp.transpose(gq * SCALE).astype(BF16)


def whole_kernel(lengths_ref, row_ref, k_ref, v_ref, qin_ref, din_ref, oo_ref, oq_ref, ok_ref, ov_ref,
                 load, info, infos, kvs, zkv, zq, zd, hots, backs, place,
                 skv, rkv, sq, rq, sd, rd, kv, kt, vt, q, o, d, gq, lse, g, landed,
                 so, ro, sg, rg, skg, rkg, zo, zg, zkg, okv, swap_s, swap_r, *sems):
    here = Here()
    core = here.core
    every = lambda part: pl.ds(0, TOK + 32)
    plain = lambda part: pl.ds(0, TOK)
    chunk = lambda part: rows48(here.chip(part))
    cs = [sems[3 * i : 3 * i + 3] for i in range(7)]
    ps = [sems[21 + 3 * i : 24 + 3 * i] for i in range(6)]
    a_info = Column(here, lambda p: info, lambda p: infos.at[p], cs[0])
    a_kv = Column(here, lambda p: kvs.at[:, cols(p * D, D)], lambda p: zkv.at[p], cs[1])
    a_q = Column(here, lambda p: qin_ref.at[:, cols(p * 512, 512)], lambda p: zq.at[p], cs[2])
    a_d = Column(here, lambda p: din_ref.at[:, cols(p * 512, 512)], lambda p: zd.at[p], cs[3])
    a_o = Column(here, lambda p: zo.at[p], lambda p: oo_ref.at[:, cols(p * 512, 512)], cs[4])
    a_g = Column(here, lambda p: zg.at[p], lambda p: oq_ref.at[:, cols(p * 512, 512)], cs[5])
    a_kg = Column(here, lambda p: zkg.at[p], lambda p: okv.at[:, cols(p * D, D)], cs[6])
    b_kv = Plane(here, skv, rkv, ps[0], every)
    b_kg = Plane(here, skg, rkg, ps[1], plain)
    b_q = Plane(here, sq, rq, ps[2], chunk)
    b_d = Plane(here, sd, rd, ps[3], chunk)
    b_o = Plane(here, so, ro, ps[4], chunk)
    b_g = Plane(here, sg, rg, ps[5], chunk)

    loads = []
    for z in range(4):
        for e, ref in enumerate((k_ref, v_ref)):
            to = kvs.at[:, pl.ds((2 * z + e) * D, D)]
            loads.append(pltpu.make_async_copy(ref.at[:, pl.ds(z * D, D)], to, load.at[2 * z + e]))
    for c in loads:
        c.start()
    dest_r = row_ref[...]
    g_r = group_of(dest_r)
    g_c = jnp.transpose(jnp.broadcast_to(g_r.astype(F32), (8, TOK)))[:, 0:1]
    same = (g_r.astype(F32) == g_c) & (iota((TOK, TOK), 0) < iota((TOK, TOK), 1))
    rank = jnp.sum(jnp.where(same, 1.0, 0.0), axis=0, keepdims=True).astype(jnp.int32) + CAP * core
    which = iota((8, TOK), 0)
    info[...] = jnp.where(
        which == 0, g_r * 48 + rank, jnp.where(which == 1, place_of(dest_r) + 1, jnp.where(which == 2, g_r, rank))
    )
    for c in loads:
        c.wait()

    greet(here)
    a_info.start()
    a_kv.start()
    a_q.start()
    a_info.finish_in()
    which = iota((16, 32, D), 1)
    tail = jnp.zeros((16, 32, D), F32)
    for pair in range(4):
        laid = jnp.zeros((16, D), F32)
        for c in (2 * pair, 2 * pair + 1):
            hots[c] = jnp.where(iota((768, TOK), 0) == infos[c, 0:1], 1.0, 0.0).astype(BF16)
            named = jnp.where(iota((16, TOK), 0) == infos[c, 2:3], infos[c, 1:2].astype(F32), 0.0).astype(BF16)
            laned = jnp.where(iota((D, TOK), 0) == infos[c, 3:4], 1.0, 0.0).astype(BF16)
            laid += dot(named, laned, NT)
        tail = jnp.where(which == pair, laid.reshape(16, 1, D), tail)
    a_kv.finish_in()
    for pair in range(4):
        pack_pair(hots, zkv, pair, skv)
    skv[:, TOK:] = tail.astype(BF16)
    b_kv.start()
    for part in INWARD:
        a_q.finish_chip(part)
        pack_pair(hots, zq, here.chip(part), sq)
        b_q.start(part)
    a_d.start()
    slot_c = jnp.transpose(jnp.concatenate([infos[c, 0:1].astype(F32) for c in range(8)], axis=0))
    for c in range(8):
        backs[c] = jnp.where(iota((TOK, 768), 1).astype(F32) == slot_c[:, c : c + 1], 1.0, 0.0).astype(BF16)

    b_kv.finish_in()
    total = jnp.zeros((8, 768), F32)
    for s in range(16):
        mine = jnp.concatenate([rkv[s, TOK : TOK + 16].astype(F32)[:8], jnp.zeros((8, 640), F32)], axis=1)
        total += mine if s == 0 else pltpu.roll(mine, 48 * s, 1)
    odd = (iota((8, 768), 1) % 48) >= CAP
    place[...] = jnp.where(odd & (total > 0.0), total + 192.0, total)
    for pair in range(4):
        kv[core, rows384(pair)] = regroup(place, rkv, pair).astype(BF16)
    partner = (here.dp, here.peer(0, 1))
    swap = remote(kv.at[core], kv.at[core], swap_s.at[0], swap_r.at[0], partner)
    swap.start()
    for part in INWARD:
        a_d.finish_chip(part)
        pack_pair(hots, zd, here.chip(part), sd)
        b_d.start(part)
    swapped = kv.at[1 - core]
    remote(swapped, swapped, swap_s.at[0], swap_r.at[0], partner).wait_recv()
    kt[...] = jnp.transpose(kv[0].astype(F32)).astype(BF16)
    vt[...] = jnp.transpose(kv[1].astype(F32)).astype(BF16)

    end = lengths_ref[0, here.dp]
    for part in INWARD:
        b_q.finish_in(part)
        pair = here.chip(part)
        x = regroup(place, rq, pair).astype(BF16)
        for h in range(4):
            q[h, rows384(pair)] = x[:, h * D : h * D + D]

    @pl.loop(0, 4)
    def _(h):
        forward_head(h, end, q, kv, vt, o, lse)

    for part in OUTWARD:
        pair = here.chip(part)
        return_pair(place, jnp.concatenate([o[h, rows384(pair)] for h in range(4)], axis=1), pair, so)
        b_o.start(part)

    swap.wait_send()
    g[...] = jnp.zeros_like(g)
    for part in INWARD:
        b_d.finish_in(part)
        pair = here.chip(part)
        x = regroup(place, rd, pair).astype(BF16)
        for h in range(4):
            d[h, rows384(pair)] = x[:, h * D : h * D + D]

    @pl.loop(0, 4)
    def _(h):
        backward_head(h, end, q, d, o, lse, kv, kt, g, gq)

    swap = remote(g.at[1 - core], landed, swap_s.at[1], swap_r.at[1], partner)
    swap.start()

    def give(part):
        pair = here.chip(part)
        return_pair(place, jnp.concatenate([gq[h, rows384(pair)] for h in range(4)], axis=1), pair, sg)
        b_g.start(part)

    give(OUTWARD[0])
    give(OUTWARD[1])
    swap.wait_recv()
    factor = jnp.where(core == 0, SCALE, 1.0).astype(F32)
    for pair in range(4):
        rows = rows384(pair)
        return_pair(place, ((g[core, rows] + landed[rows]) * factor).astype(BF16), pair, skg)
    b_kg.start()
    for part in OUTWARD:
        b_o.finish_in(part)
        unpack_pair(backs, ro, here.chip(part), zo)
        a_o.start_chip(part)
    give(OUTWARD[2])
    give(OUTWARD[3])
    for part in OUTWARD[:2]:
        b_g.finish_in(part)
        unpack_pair(backs, rg, here.chip(part), zg)
        a_g.start_chip(part)
    b_kg.finish_in()
    for pair in range(4):
        unpack_pair(backs, rkg, pair, zkg)
    a_kg.start()
    for part in OUTWARD[2:]:
        b_g.finish_in(part)
        unpack_pair(backs, rg, here.chip(part), zg)
        a_g.start_chip(part)
    a_kg.finish_in()
    for z in range(4):
        ok_ref[:, z * D : z * D + D] = okv[:, 2 * z * D : 2 * z * D + D]
        ov_ref[:, z * D : z * D + D] = okv[:, 2 * z * D + D : 2 * z * D + 2 * D]
    a_o.finish_in()
    a_g.finish_in()
    swap.wait_send()
    for c in (a_info, a_kv, a_q, a_d, a_o, a_g, a_kg, b_kv, b_kg, b_q, b_d, b_o, b_g):
        c.finish_out()


def local(queries, keys, values, grad_out, destination, lengths):
    slots, wide = (16, TOK, 512), (8, TOK, 512)
    scratch = [
        ((8, TOK), jnp.int32), ((8, 8, TOK), jnp.int32), ((TOK, 1024), BF16), ((8, TOK, D), BF16), (wide, BF16), (wide, BF16),
        ((8, 768, TOK), BF16), ((8, TOK, 768), BF16), ((8, 768), F32),
        ((16, TOK + 32, D), BF16), ((16, TOK + 32, D), BF16), (slots, BF16), (slots, BF16), (slots, BF16), (slots, BF16),
        ((2, 1536, D), BF16), ((D, 1536), BF16), ((D, 1536), BF16),
        ((4, 1536, D), BF16), ((4, 1536, D), BF16), ((4, 1536, D), BF16), ((4, 1536, D), BF16), ((4, 1, 1536), F32),
        ((2, 1536, D), F32), ((1536, D), F32),
        (slots, BF16), (slots, BF16), (slots, BF16), (slots, BF16), ((16, TOK, D), BF16), ((16, TOK, D), BF16),
        (wide, BF16), (wide, BF16), ((8, TOK, D), BF16), ((TOK, 1024), BF16),
    ]
    return pl.pallas_call(
        whole_kernel,
        out_shape=(
            jax.ShapeDtypeStruct((TOK, 4096), BF16),
            jax.ShapeDtypeStruct((TOK, 4096), BF16),
            jax.ShapeDtypeStruct((TOK, 512), BF16),
            jax.ShapeDtypeStruct((TOK, 512), BF16),
        ),
        in_specs=[SMEM, VMEM] + [HBM] * 4,
        out_specs=(HBM, HBM, VMEM, VMEM),
        scratch_shapes=[DMA((8,))]
        + [pltpu.VMEM(shape, dtype) for shape, dtype in scratch]
        + [DMA((2,)), DMA((2,))]
        + Column.scratch() * 7
        + Plane.scratch(1) * 2 + Plane.scratch(4) * 4,
        compiler_params=pltpu.CompilerParams(collective_id=0, has_side_effects=True, vmem_limit_bytes=60 << 20),
        name="whole",
    )(lengths.T, destination.reshape(1, TOK), keys, values, queries, grad_out)


def solution(mesh):
    rows = P(("dp", "ctx"), None)
    return jax.shard_map(
        local,
        mesh=mesh,
        in_specs=(rows, rows, rows, rows, P(("dp", "ctx")), P()),
        out_specs=(rows, rows, rows, rows),
        check_vma=False,
    )
```

```python
import functools
import math

import jax
import jax.numpy as jnp
from jax import lax
from jax.experimental import pallas as pl
from jax.experimental.pallas import tpu as pltpu
from jax.sharding import PartitionSpec as P

D = 128
TOK = 192
CAP = 24
F32 = jnp.float32
BF16 = jnp.bfloat16
MESH = pl.DeviceIdType.MESH
VMEM = pl.BlockSpec(memory_space=pltpu.VMEM)
SMEM = pl.BlockSpec(memory_space=pltpu.SMEM)
HBM = pl.BlockSpec(memory_space=pltpu.HBM)
DMA = pltpu.SemaphoreType.DMA
NN = (((1,), (0,)), ((), ()))
NT = (((1,), (1,)), ((), ()))
TN = (((0,), (0,)), ((), ()))
TILE = 256
SCALE = 1.0 / math.sqrt(D)
EXP2 = SCALE * math.log2(math.e)


def dot(a, b, dims=NN):
    return lax.dot_general(a, b, dims, preferred_element_type=F32)


def iota(shape, axis):
    return lax.broadcasted_iota(jnp.int32, shape, axis)


def group_of(dest):
    return ((dest >> 9) * 43) >> 7


def place_of(dest):
    return dest - 192 * (((dest >> 6) * 171) >> 9)


STEPS = [(1, 0), (-1, 0), (0, 1), (0, -1), (2, 0), (0, 2), (1, 1), (-1, -1), (1, -1), (-1, 1),
         (2, 1), (1, 2), (2, -1), (-1, 2), (2, 2)]
FAR_FIRST = (2, 1, 3, 0)


class Here:
    def __init__(self):
        self.dp = lax.axis_index("dp")
        self.ctx = lax.axis_index("ctx")
        self.x, self.y = self.dp // 4, self.dp % 4
        self.z, self.core = self.ctx // 2, self.ctx % 2

    def at(self, dx, dy):
        return ((self.x + (dx + 4)) % 4) * 4 + (self.y + (dy + 4)) % 4

    def chip(self, dz):
        return (self.z + (dz + 4)) % 4

    def peer(self, dz, other):
        return self.chip(dz) * 2 + (self.core + other) % 2


def greet(here):
    barrier = pltpu.get_barrier_semaphore()
    who = [(here.at(*step), here.ctx) for step in STEPS] + [(here.dp, here.peer(*step)) for step in COLUMN[1:]]
    for device in who:
        pl.semaphore_signal(barrier, inc=1, device_id=device, device_id_type=MESH)
    pl.semaphore_wait(barrier, len(who))


def remote(src, dst, send_sem, recv_sem, device):
    return pltpu.make_async_remote_copy(
        src_ref=src, dst_ref=dst, send_sem=send_sem, recv_sem=recv_sem, device_id=device, device_id_type=MESH
    )


class Plane:
    @staticmethod
    def scratch():
        return [DMA((15,)), DMA((15,)), DMA]

    def __init__(self, here, source, target, scratch):
        self.here, self.source, self.target = here, source, target
        self.send_s, self.recv_s, self.own_s = scratch
        self.own = pltpu.make_async_copy(source(here.dp), target(here.dp), self.own_s)
        self.begun = []

    def start_step(self, i):
        to = self.here.at(*STEPS[i])
        c = remote(self.source(to), self.target(self.here.dp), self.send_s.at[i], self.recv_s.at[i], (to, self.here.ctx))
        c.start()
        self.begun.append(c)

    def start(self):
        for i in range(15):
            self.start_step(i)
        self.own.start()

    def finish_in(self):
        for i, (dx, dy) in enumerate(STEPS):
            source = self.here.at(-dx, -dy)
            landing = self.target(source)
            remote(landing, landing, self.send_s.at[i], self.recv_s.at[i], (source, self.here.ctx)).wait_recv()
        self.own.wait()

    def finish_out(self):
        for c in self.begun:
            c.wait_send()


COLUMN = [(0, 0), (0, 1), (1, 0), (1, 1), (3, 0), (3, 1), (2, 0), (2, 1)]


class Column:
    @staticmethod
    def scratch():
        return [DMA((8,)), DMA((8,)), DMA]

    def __init__(self, here, source, target, scratch):
        self.here, self.source, self.target = here, source, target
        self.send_s, self.recv_s, self.own_s = scratch
        self.own = pltpu.make_async_copy(source(here.ctx), target(here.ctx), self.own_s)
        self.begun = []

    def start_to(self, dz, other):
        if (dz, other) == (0, 0):
            self.own.start()
            return
        to, n = self.here.peer(dz, other), 2 * dz + other
        c = remote(self.source(to), self.target(self.here.ctx), self.send_s.at[n], self.recv_s.at[n], (self.here.dp, to))
        c.start()
        self.begun.append(c)

    def start(self):
        for dz in FAR_FIRST:
            for other in range(2):
                self.start_to(dz, other)

    def finish_chip(self, dz):
        for other in range(2):
            n = 2 * ((4 - dz) % 4) + other
            if n == 0:
                self.own.wait()
                continue
            origin = self.here.peer(dz, other)
            landing = self.target(origin)
            remote(landing, landing, self.send_s.at[n], self.recv_s.at[n], (self.here.dp, origin)).wait_recv()

    def finish_in(self):
        for dz in range(4):
            self.finish_chip(dz)

    def finish_out(self):
        for c in self.begun:
            c.wait_send()


def cols(start, width):
    return pl.ds(pl.multiple_of(start, 128), width)


def rows192(c):
    return pl.ds(pl.multiple_of(192 * c, 64), 192)


def rows48(pair):
    return pl.ds(pl.multiple_of(48 * pair, 16), 48)


def put_in_order(here, exchange, got, opens, hots, slots, out):
    for s in range(16):
        slots[s] = dot(opens[s], got[s]).astype(BF16)
    for dz in FAR_FIRST:
        for other in range(2):
            pair = here.peer(dz, other)
            x = dot(hots[pair], slots[:, rows48(pair)].reshape(768, D))
            out[pair] = x.astype(BF16).reshape(2, TOK, D)
            exchange.start_to(dz, other)


def put_back(here, exchange, got, backs, hots_t, slots, out):
    for pair in range(8):
        x = dot(hots_t[pair], got[pair].reshape(384, D)).astype(BF16)
        slots[:, rows48(pair)] = x.reshape(16, 48, D)
    for i, step in enumerate(STEPS):
        s = here.at(*step)
        out[s] = dot(backs[s], slots[s]).astype(BF16)
        exchange.start_step(i)
    out[here.dp] = dot(backs[here.dp], slots[here.dp]).astype(BF16)
    exchange.own.start()


def tiles():
    for j in range(6):
        low = 0 if j < 4 else 512
        yield j, list(range(low, (j + 1) * TILE, TILE))


def allowed(j, k, end):
    diagonal, mixed = k == j * TILE, j >= 2
    if not diagonal and not mixed:
        return None
    kp = k + iota((TILE, TILE), 0)
    qp = j * TILE + iota((1, TILE), 1)
    mask = None
    if mixed:
        mask = kp >= jnp.where(qp >= end, end, 0)
    if diagonal:
        causal = kp <= qp
        mask = causal if mask is None else mask & causal
    return mask


def forward_unit(e, end, q_ref, k_ref, vt_ref, o_ref, lse_ref):
    for j, ks in tiles():
        rows = slice(j * TILE, j * TILE + TILE)
        q = q_ref[e, rows]
        scores = []
        for k in ks:
            s = dot(k_ref[e, k : k + TILE], q, NT)
            mask = allowed(j, k, end)
            scores.append(s if mask is None else jnp.where(mask, s, -jnp.inf))
        top = jnp.max(functools.reduce(jnp.maximum, scores), axis=0, keepdims=True)
        expo = [jnp.exp2((s - top) * EXP2) for s in scores]
        total = jnp.sum(functools.reduce(jnp.add, expo), axis=0, keepdims=True)
        inverse = 1.0 / total
        att = jnp.zeros((D, TILE), F32)
        for k, x in zip(ks, expo):
            att += dot(vt_ref[e, :, k : k + TILE], (x * inverse).astype(BF16))
        o_ref[e, rows] = jnp.transpose(att).astype(BF16)
        lse_ref[e, :, rows] = top * EXP2 + jnp.log2(total)


def backward_unit(e, end, q_ref, d_ref, o_ref, lse_ref, k_ref, v_ref, kt_ref, gk_ref, gv_ref, gq_ref):
    for j, ks in tiles():
        rows = slice(j * TILE, j * TILE + TILE)
        q, d = q_ref[e, rows], d_ref[e, rows]
        product = d.astype(F32) * o_ref[e, rows].astype(F32)
        delta = jnp.sum(jnp.transpose(product), axis=0, keepdims=True)
        lse = lse_ref[e, :, rows]
        gq = jnp.zeros((D, TILE), F32)
        for k in ks:
            keys = slice(k, k + TILE)
            p = jnp.exp2(dot(k_ref[e, keys], q, NT) * EXP2 - lse)
            mask = allowed(j, k, end)
            if mask is not None:
                p = jnp.where(mask, p, 0.0)
            dp = dot(v_ref[e, keys], d, NT)
            ds = (p * (dp - delta)).astype(BF16)
            gv_ref[e, keys] += dot(p.astype(BF16), d)
            gk_ref[e, keys] += dot(ds, q)
            gq += dot(kt_ref[e, :, keys], ds)
        gq_ref[e, rows] = jnp.transpose(gq * SCALE).astype(BF16)


def whole_kernel(lengths_ref, row_ref, k_ref, v_ref, q_ref, d_ref, oo_ref, oq_ref, ok_ref, ov_ref,
                 info, infos, place, opens, backs, hots, hots_t, slots, got, sent, here_in, here_out, back, ready,
                 kt, vt, lse, gk, gv, parts, *sems):
    here = Here()
    p = here.dp
    sems = [sems[3 * i : 3 * i + 3] for i in range(25)]

    def head_of(ref, h):
        return lambda t: ref.at[:, cols(t * 256 + h * D, D)]

    def kv_head_of(ref):
        return lambda t: ref.at[:, cols((t // 4) * D, D)]

    inward = [kv_head_of(k_ref), kv_head_of(v_ref), head_of(q_ref, 0), head_of(d_ref, 0), head_of(q_ref, 1), head_of(d_ref, 1)]
    p_info = Plane(here, lambda t: info, lambda t: infos.at[t], sems[24])
    p_in = [Plane(here, inward[n], lambda t, n=n: got.at[n, t], sems[n]) for n in range(6)]
    c_in = [Column(here, lambda c, n=n: sent.at[n, c], lambda c, n=n: here_in.at[n, :, rows192(c)], sems[6 + n]) for n in range(6)]
    outward = [head_of(oo_ref, 0), head_of(oq_ref, 0), head_of(oo_ref, 1), head_of(oq_ref, 1)]
    outward += [lambda t: parts.at[0, t], lambda t: parts.at[1, t]]
    c_out = [Column(here, lambda c, n=n: here_out.at[n, :, rows192(c)], lambda c, n=n: back.at[n, c], sems[12 + n]) for n in range(6)]
    p_out = [Plane(here, lambda t, n=n: ready.at[n, t], outward[n], sems[18 + n]) for n in range(6)]

    dest_r = row_ref[...]
    g_r = group_of(dest_r)
    g_c = jnp.transpose(jnp.broadcast_to(g_r.astype(F32), (8, TOK)))[:, 0:1]
    same = (g_r.astype(F32) == g_c) & (iota((TOK, TOK), 0) < iota((TOK, TOK), 1))
    rank = jnp.sum(jnp.where(same, 1.0, 0.0), axis=0, keepdims=True).astype(jnp.int32)
    which = iota((8, TOK), 0)
    info[...] = jnp.where(
        which == 0,
        g_r * CAP + rank,
        jnp.where(which == 1, place_of(dest_r) + 1, jnp.where(which == 2, g_r >> 1, rank + CAP * (g_r & 1))),
    )

    greet(here)
    p_info.start()
    for x in p_in:
        x.start()

    p_info.finish_in()
    total = jnp.zeros((8, 768), F32)
    for s in range(16):
        opens[s] = jnp.where(iota((384, TOK), 0) == infos[s, 0:1], 1.0, 0.0).astype(BF16)
        named = jnp.where(iota((8, TOK), 0) == infos[s, 2:3], infos[s, 1:2].astype(F32), 0.0).astype(BF16)
        laned = jnp.where(iota((D, TOK), 0) == infos[s, 3:4], 1.0, 0.0).astype(BF16)
        mine = jnp.concatenate([dot(named, laned, NT), jnp.zeros((8, 640), F32)], axis=1)
        total += mine if s == 0 else pltpu.roll(mine, 48 * s, 1)
    odd = (iota((8, 768), 1) % 48) >= CAP
    place[...] = jnp.where(odd & (total > 0.0), total + 192.0, total)

    def hot_of(pair):
        return jnp.where(place[pair : pair + 1] == (iota((384, 768), 0) + 1).astype(F32), 1.0, 0.0)

    for pair in range(8):
        hots[pair] = hot_of(pair).astype(BF16)

    def order(n):
        p_in[n].finish_in()
        put_in_order(here, c_in[n], got.at[n], opens, hots, slots, sent.at[n])

    order(0)
    order(1)
    slot_c = jnp.transpose(jnp.concatenate([infos[s, 0:1].astype(F32) for s in range(16)], axis=0))
    for s in range(16):
        backs[s] = jnp.where(iota((TOK, 384), 1).astype(F32) == slot_c[:, s : s + 1], 1.0, 0.0).astype(BF16)
    order(2)
    for pair in range(8):
        hots_t[pair] = jnp.transpose(hot_of(pair)).astype(BF16)
    order(3)
    for n, turned in enumerate((kt, vt)):
        c_in[n].finish_in()
        for e in range(2):
            turned[e] = jnp.transpose(here_in[n, e].astype(F32)).astype(BF16)
    gk[...] = jnp.zeros_like(gk)
    gv[...] = jnp.zeros_like(gv)

    def end_of(e):
        return lengths_ref[0, 2 * here.ctx + e]

    def forward(h):
        c_in[2 + 2 * h].finish_in()

        @pl.loop(0, 2)
        def _(e):
            forward_unit(e, end_of(e), here_in.at[2 + 2 * h], here_in.at[0], vt, here_out.at[2 * h], lse.at[h])

        c_out[2 * h].start()

    def backward(h, e):
        backward_unit(e, end_of(e), here_in.at[2 + 2 * h], here_in.at[3 + 2 * h], here_out.at[2 * h], lse.at[h],
                      here_in.at[0], here_in.at[1], kt, gk, gv, here_out.at[1 + 2 * h])

    def restore(n):
        c_out[n].finish_in()
        put_back(here, p_out[n], back.at[n], backs, hots_t, slots, ready.at[n])

    forward(0)
    order(4)
    c_in[3].finish_in()
    backward(0, 0)
    order(5)
    backward(0, 1)
    c_out[1].start()
    forward(1)
    restore(0)
    c_in[5].finish_in()
    backward(1, 0)
    restore(1)
    backward(1, 1)
    c_out[3].start()
    here_out[4] = (gk[...] * SCALE).astype(BF16)
    c_out[4].start()
    here_out[5] = gv[...].astype(BF16)
    c_out[5].start()
    for n in (2, 3, 4, 5):
        restore(n)
    for n, out in enumerate((ok_ref, ov_ref)):
        p_out[4 + n].finish_in()
        for x in range(4):
            added = parts[n, 4 * x].astype(F32)
            for y in range(1, 4):
                added += parts[n, 4 * x + y].astype(F32)
            out[:, x * D : x * D + D] = added.astype(BF16)
    for x in p_out[:4]:
        x.finish_in()
    for x in [p_info] + p_in + c_in + c_out + p_out:
        x.finish_out()


def local(queries, keys, values, grad_out, destination, lengths):
    scratch = [
        ((8, TOK), jnp.int32), ((16, 8, TOK), jnp.int32), ((8, 768), F32),
        ((16, 384, TOK), BF16), ((16, TOK, 384), BF16), ((8, 384, 768), BF16), ((8, 768, 384), BF16), ((16, 384, D), BF16),
        ((6, 16, TOK, D), BF16), ((6, 8, 2, TOK, D), BF16), ((6, 2, 1536, D), BF16),
        ((6, 2, 1536, D), BF16), ((6, 8, 2, TOK, D), BF16), ((6, 16, TOK, D), BF16),
        ((2, D, 1536), BF16), ((2, D, 1536), BF16), ((2, 2, 1, 1536), F32),
        ((2, 1536, D), F32), ((2, 1536, D), F32), ((2, 16, TOK, D), BF16),
    ]
    return pl.pallas_call(
        whole_kernel,
        out_shape=(
            jax.ShapeDtypeStruct((TOK, 4096), BF16),
            jax.ShapeDtypeStruct((TOK, 4096), BF16),
            jax.ShapeDtypeStruct((TOK, 512), BF16),
            jax.ShapeDtypeStruct((TOK, 512), BF16),
        ),
        in_specs=[SMEM, VMEM] + [HBM] * 4,
        out_specs=(HBM, HBM, VMEM, VMEM),
        scratch_shapes=[pltpu.VMEM(shape, dtype) for shape, dtype in scratch]
        + Plane.scratch() * 6 + Column.scratch() * 12 + Plane.scratch() * 7,
        compiler_params=pltpu.CompilerParams(collective_id=0, has_side_effects=True, vmem_limit_bytes=60 << 20),
        name="whole",
    )(lengths.T, destination.reshape(1, TOK), keys, values, queries, grad_out)


def solution(mesh):
    rows = P(("dp", "ctx"), None)
    return jax.shard_map(
        local,
        mesh=mesh,
        in_specs=(rows, rows, rows, rows, P(("dp", "ctx")), P()),
        out_specs=(rows, rows, rows, rows),
        check_vma=False,
    )
```

```python
import functools
import math

import jax
import jax.numpy as jnp
from jax import lax
from jax.experimental import pallas as pl
from jax.experimental.pallas import tpu as pltpu
from jax.sharding import PartitionSpec as P

D = 128
TOK = 192
CAP = 24
F32 = jnp.float32
BF16 = jnp.bfloat16
MESH = pl.DeviceIdType.MESH
VMEM = pl.BlockSpec(memory_space=pltpu.VMEM)
SMEM = pl.BlockSpec(memory_space=pltpu.SMEM)
HBM = pl.BlockSpec(memory_space=pltpu.HBM)
DMA = pltpu.SemaphoreType.DMA
NN = (((1,), (0,)), ((), ()))
NT = (((1,), (1,)), ((), ()))
TN = (((0,), (0,)), ((), ()))
TILE = 256
SCALE = 1.0 / math.sqrt(D)
EXP2 = SCALE * math.log2(math.e)


def dot(a, b, dims=NN):
    return lax.dot_general(a, b, dims, preferred_element_type=F32)


def iota(shape, axis):
    return lax.broadcasted_iota(jnp.int32, shape, axis)


def group_of(dest):
    return ((dest >> 9) * 43) >> 7


def place_of(dest):
    return dest - 192 * (((dest >> 6) * 171) >> 9)


STEPS = [(1, 0), (-1, 0), (0, 1), (0, -1), (2, 0), (0, 2), (1, 1), (-1, -1), (1, -1), (-1, 1),
         (2, 1), (1, 2), (2, -1), (-1, 2), (2, 2)]
FAR_FIRST = (2, 1, 3, 0)


class Here:
    def __init__(self):
        self.dp = lax.axis_index("dp")
        self.ctx = lax.axis_index("ctx")
        self.x, self.y = self.dp // 4, self.dp % 4
        self.z, self.core = self.ctx // 2, self.ctx % 2

    def at(self, dx, dy):
        return ((self.x + (dx + 4)) % 4) * 4 + (self.y + (dy + 4)) % 4

    def chip(self, dz):
        return (self.z + (dz + 4)) % 4

    def peer(self, dz, other):
        return self.chip(dz) * 2 + (self.core + other) % 2


def greet(here):
    barrier = pltpu.get_barrier_semaphore()
    who = [(here.at(*step), here.ctx) for step in STEPS] + [(here.dp, here.peer(*step)) for step in COLUMN[1:]]
    for device in who:
        pl.semaphore_signal(barrier, inc=1, device_id=device, device_id_type=MESH)
    pl.semaphore_wait(barrier, len(who))


def remote(src, dst, send_sem, recv_sem, device):
    return pltpu.make_async_remote_copy(
        src_ref=src, dst_ref=dst, send_sem=send_sem, recv_sem=recv_sem, device_id=device, device_id_type=MESH
    )


class Plane:
    @staticmethod
    def scratch():
        return [DMA((15,)), DMA((15,)), DMA]

    def __init__(self, here, source, target, scratch):
        self.here, self.source, self.target = here, source, target
        self.send_s, self.recv_s, self.own_s = scratch
        self.own = pltpu.make_async_copy(source(here.dp), target(here.dp), self.own_s)
        self.begun = []

    def start_step(self, i):
        to = self.here.at(*STEPS[i])
        c = remote(self.source(to), self.target(self.here.dp), self.send_s.at[i], self.recv_s.at[i], (to, self.here.ctx))
        c.start()
        self.begun.append(c)

    def start(self):
        for i in range(15):
            self.start_step(i)
        self.own.start()

    def finish_in(self):
        for i, (dx, dy) in enumerate(STEPS):
            source = self.here.at(-dx, -dy)
            landing = self.target(source)
            remote(landing, landing, self.send_s.at[i], self.recv_s.at[i], (source, self.here.ctx)).wait_recv()
        self.own.wait()

    def finish_out(self):
        for c in self.begun:
            c.wait_send()


COLUMN = [(0, 0), (0, 1), (1, 0), (1, 1), (3, 0), (3, 1), (2, 0), (2, 1)]


class Column:
    @staticmethod
    def scratch():
        return [DMA((8,)), DMA((8,)), DMA]

    def __init__(self, here, source, target, scratch):
        self.here, self.source, self.target = here, source, target
        self.send_s, self.recv_s, self.own_s = scratch
        self.own = pltpu.make_async_copy(source(here.ctx), target(here.ctx), self.own_s)
        self.begun = []

    def start_to(self, dz, other):
        if (dz, other) == (0, 0):
            self.own.start()
            return
        to, n = self.here.peer(dz, other), 2 * dz + other
        c = remote(self.source(to), self.target(self.here.ctx), self.send_s.at[n], self.recv_s.at[n], (self.here.dp, to))
        c.start()
        self.begun.append(c)

    def start(self):
        for dz in FAR_FIRST:
            for other in range(2):
                self.start_to(dz, other)

    def finish_chip(self, dz):
        for other in range(2):
            n = 2 * ((4 - dz) % 4) + other
            if n == 0:
                self.own.wait()
                continue
            origin = self.here.peer(dz, other)
            landing = self.target(origin)
            remote(landing, landing, self.send_s.at[n], self.recv_s.at[n], (self.here.dp, origin)).wait_recv()

    def finish_in(self):
        for dz in range(4):
            self.finish_chip(dz)

    def finish_out(self):
        for c in self.begun:
            c.wait_send()


def cols(start, width):
    return pl.ds(pl.multiple_of(start, 128), width)


def rows192(c):
    return pl.ds(pl.multiple_of(192 * c, 64), 192)


def rows48(pair):
    return pl.ds(pl.multiple_of(48 * pair, 16), 48)


def put_in_order(here, exchange, got, opens, hots, slots, out):
    for s in range(16):
        slots[s] = dot(opens[s], got[s]).astype(BF16)
    for dz in FAR_FIRST:
        for other in range(2):
            pair = here.peer(dz, other)
            x = dot(hots[pair], slots[:, rows48(pair)].reshape(768, D))
            out[pair] = x.astype(BF16).reshape(2, TOK, D)
            exchange.start_to(dz, other)


def put_back(here, exchange, got, backs, hots_t, slots, out):
    for pair in range(8):
        x = dot(hots_t[pair], got[pair].reshape(384, D)).astype(BF16)
        slots[:, rows48(pair)] = x.reshape(16, 48, D)
    for i, step in enumerate(STEPS):
        s = here.at(*step)
        out[s] = dot(backs[s], slots[s]).astype(BF16)
        exchange.start_step(i)
    out[here.dp] = dot(backs[here.dp], slots[here.dp]).astype(BF16)
    exchange.own.start()


def tiles():
    for j in range(6):
        low = 0 if j < 4 else 512
        yield j, list(range(low, (j + 1) * TILE, TILE))


def allowed(j, k, end):
    diagonal, mixed = k == j * TILE, j >= 2
    if not diagonal and not mixed:
        return None
    kp = k + iota((TILE, TILE), 0)
    qp = j * TILE + iota((1, TILE), 1)
    mask = None
    if mixed:
        mask = kp >= jnp.where(qp >= end, end, 0)
    if diagonal:
        causal = kp <= qp
        mask = causal if mask is None else mask & causal
    return mask


def forward_unit(e, end, q_ref, k_ref, vt_ref, o_ref, lse_ref):
    for j, ks in tiles():
        rows = slice(j * TILE, j * TILE + TILE)
        q = q_ref[e, rows]
        scores = []
        for k in ks:
            s = dot(k_ref[e, k : k + TILE], q, NT)
            mask = allowed(j, k, end)
            scores.append(s if mask is None else jnp.where(mask, s, -jnp.inf))
        top = jnp.max(functools.reduce(jnp.maximum, scores), axis=0, keepdims=True)
        expo = [jnp.exp2((s - top) * EXP2) for s in scores]
        total = jnp.sum(functools.reduce(jnp.add, expo), axis=0, keepdims=True)
        inverse = 1.0 / total
        att = jnp.zeros((D, TILE), F32)
        for k, x in zip(ks, expo):
            att += dot(vt_ref[e, :, k : k + TILE], (x * inverse).astype(BF16))
        o_ref[e, rows] = jnp.transpose(att).astype(BF16)
        lse_ref[e, :, rows] = top * EXP2 + jnp.log2(total)


def backward_unit(e, end, q_ref, d_ref, o_ref, lse_ref, k_ref, v_ref, kt_ref, gk_ref, gv_ref, gq_ref):
    for j, ks in tiles():
        rows = slice(j * TILE, j * TILE + TILE)
        q, d = q_ref[e, rows], d_ref[e, rows]
        product = d.astype(F32) * o_ref[e, rows].astype(F32)
        delta = jnp.sum(jnp.transpose(product), axis=0, keepdims=True)
        lse = lse_ref[e, :, rows]
        gq = jnp.zeros((D, TILE), F32)
        for k in ks:
            keys = slice(k, k + TILE)
            p = jnp.exp2(dot(k_ref[e, keys], q, NT) * EXP2 - lse)
            mask = allowed(j, k, end)
            if mask is not None:
                p = jnp.where(mask, p, 0.0)
            dp = dot(v_ref[e, keys], d, NT)
            ds = (p * (dp - delta)).astype(BF16)
            gv_ref[e, keys] += dot(p.astype(BF16), d)
            gk_ref[e, keys] += dot(ds, q)
            gq += dot(kt_ref[e, :, keys], ds)
        gq_ref[e, rows] = jnp.transpose(gq * SCALE).astype(BF16)


def whole_kernel(lengths_ref, row_ref, k_ref, v_ref, q_ref, d_ref, oo_ref, oq_ref, ok_ref, ov_ref,
                 info, infos, place, opens, backs, hots, hots_t, slots, got, sent, here_in, here_out, back, ready,
                 kt, vt, lse, gk, gv, parts, *sems):
    here = Here()
    p = here.dp
    sems = [sems[3 * i : 3 * i + 3] for i in range(25)]

    def head_of(ref, h):
        return lambda t: ref.at[:, cols(t * 256 + h * D, D)]

    def kv_head_of(ref):
        return lambda t: ref.at[:, cols((t // 4) * D, D)]

    inward = [kv_head_of(k_ref), kv_head_of(v_ref), head_of(q_ref, 0), head_of(d_ref, 0), head_of(q_ref, 1), head_of(d_ref, 1)]
    p_info = Plane(here, lambda t: info, lambda t: infos.at[t], sems[24])
    p_in = [Plane(here, inward[n], lambda t, n=n: got.at[n, t], sems[n]) for n in range(6)]
    c_in = [Column(here, lambda c, n=n: sent.at[n, c], lambda c, n=n: here_in.at[n, :, rows192(c)], sems[6 + n]) for n in range(6)]
    outward = [head_of(oo_ref, 0), head_of(oq_ref, 0), head_of(oo_ref, 1), head_of(oq_ref, 1)]
    outward += [lambda t: parts.at[0, t], lambda t: parts.at[1, t]]
    c_out = [Column(here, lambda c, n=n: here_out.at[n, :, rows192(c)], lambda c, n=n: back.at[n, c], sems[12 + n]) for n in range(6)]
    p_out = [Plane(here, lambda t, n=n: ready.at[n, t], outward[n], sems[18 + n]) for n in range(6)]

    dest_r = row_ref[...]
    g_r = group_of(dest_r)
    g_c = jnp.transpose(jnp.broadcast_to(g_r.astype(F32), (8, TOK)))[:, 0:1]
    same = (g_r.astype(F32) == g_c) & (iota((TOK, TOK), 0) < iota((TOK, TOK), 1))
    rank = jnp.sum(jnp.where(same, 1.0, 0.0), axis=0, keepdims=True).astype(jnp.int32)
    which = iota((8, TOK), 0)
    info[...] = jnp.where(
        which == 0,
        g_r * CAP + rank,
        jnp.where(which == 1, place_of(dest_r) + 1, jnp.where(which == 2, g_r >> 1, rank + CAP * (g_r & 1))),
    )

    greet(here)
    p_info.start()
    for n in range(3):
        p_in[n].start()

    p_info.finish_in()
    total = jnp.zeros((8, 768), F32)
    for s in range(16):
        opens[s] = jnp.where(iota((384, TOK), 0) == infos[s, 0:1], 1.0, 0.0).astype(BF16)
        named = jnp.where(iota((8, TOK), 0) == infos[s, 2:3], infos[s, 1:2].astype(F32), 0.0).astype(BF16)
        laned = jnp.where(iota((D, TOK), 0) == infos[s, 3:4], 1.0, 0.0).astype(BF16)
        mine = jnp.concatenate([dot(named, laned, NT), jnp.zeros((8, 640), F32)], axis=1)
        total += mine if s == 0 else pltpu.roll(mine, 48 * s, 1)
    odd = (iota((8, 768), 1) % 48) >= CAP
    place[...] = jnp.where(odd & (total > 0.0), total + 192.0, total)

    def hot_of(pair):
        return jnp.where(place[pair : pair + 1] == (iota((384, 768), 0) + 1).astype(F32), 1.0, 0.0)

    for pair in range(8):
        hots[pair] = hot_of(pair).astype(BF16)

    def order(n):
        p_in[n].finish_in()
        if n < 3:
            p_in[n + 3].start()
        put_in_order(here, c_in[n], got.at[n], opens, hots, slots, sent.at[n])

    order(0)
    order(1)
    slot_c = jnp.transpose(jnp.concatenate([infos[s, 0:1].astype(F32) for s in range(16)], axis=0))
    for s in range(16):
        backs[s] = jnp.where(iota((TOK, 384), 1).astype(F32) == slot_c[:, s : s + 1], 1.0, 0.0).astype(BF16)
    order(2)
    place_c = jnp.transpose(place[...])
    for pair in range(8):
        slot_of = (iota((768, 384), 1) + 1).astype(F32) == place_c[:, pair : pair + 1]
        hots_t[pair] = jnp.where(slot_of, 1.0, 0.0).astype(BF16)
    order(3)
    for n, turned in enumerate((kt, vt)):
        c_in[n].finish_in()
        for e in range(2):
            turned[e] = jnp.transpose(here_in[n, e].astype(F32)).astype(BF16)
    gk[...] = jnp.zeros_like(gk)
    gv[...] = jnp.zeros_like(gv)

    def end_of(e):
        return lengths_ref[0, 2 * here.ctx + e]

    def forward(h):
        c_in[2 + 2 * h].finish_in()

        @pl.loop(0, 2)
        def _(e):
            forward_unit(e, end_of(e), here_in.at[2 + 2 * h], here_in.at[0], vt, here_out.at[2 * h], lse.at[h])

        c_out[2 * h].start()

    def backward(h, e):
        backward_unit(e, end_of(e), here_in.at[2 + 2 * h], here_in.at[3 + 2 * h], here_out.at[2 * h], lse.at[h],
                      here_in.at[0], here_in.at[1], kt, gk, gv, here_out.at[1 + 2 * h])

    def restore(n):
        c_out[n].finish_in()
        put_back(here, p_out[n], back.at[n], backs, hots_t, slots, ready.at[n])

    forward(0)
    order(4)
    c_in[3].finish_in()
    backward(0, 0)
    order(5)
    backward(0, 1)
    c_out[1].start()
    forward(1)
    restore(0)
    c_in[5].finish_in()
    backward(1, 0)
    restore(1)
    backward(1, 1)
    c_out[3].start()
    here_out[4] = (gk[...] * SCALE).astype(BF16)
    c_out[4].start()
    here_out[5] = gv[...].astype(BF16)
    c_out[5].start()
    for n in (2, 3, 4, 5):
        restore(n)
    for n, out in enumerate((ok_ref, ov_ref)):
        p_out[4 + n].finish_in()
        for x in range(4):
            added = parts[n, 4 * x].astype(F32)
            for y in range(1, 4):
                added += parts[n, 4 * x + y].astype(F32)
            out[:, x * D : x * D + D] = added.astype(BF16)
    for x in p_out[:4]:
        x.finish_in()
    for x in [p_info] + p_in + c_in + c_out + p_out:
        x.finish_out()


def local(queries, keys, values, grad_out, destination, lengths):
    scratch = [
        ((8, TOK), jnp.int32), ((16, 8, TOK), jnp.int32), ((8, 768), F32),
        ((16, 384, TOK), BF16), ((16, TOK, 384), BF16), ((8, 384, 768), BF16), ((8, 768, 384), BF16), ((16, 384, D), BF16),
        ((6, 16, TOK, D), BF16), ((6, 8, 2, TOK, D), BF16), ((6, 2, 1536, D), BF16),
        ((6, 2, 1536, D), BF16), ((6, 8, 2, TOK, D), BF16), ((6, 16, TOK, D), BF16),
        ((2, D, 1536), BF16), ((2, D, 1536), BF16), ((2, 2, 1, 1536), F32),
        ((2, 1536, D), F32), ((2, 1536, D), F32), ((2, 16, TOK, D), BF16),
    ]
    results = pl.pallas_call(
        whole_kernel,
        out_shape=(
            jax.ShapeDtypeStruct((TOK, 4096), BF16),
            jax.ShapeDtypeStruct((TOK, 4096), BF16),
            jax.ShapeDtypeStruct((TOK, 512), BF16),
            jax.ShapeDtypeStruct((TOK, 512), BF16),
        ),
        in_specs=[SMEM, VMEM] + [HBM] * 4,
        out_specs=(HBM, HBM, VMEM, VMEM),
        scratch_shapes=[pltpu.VMEM(shape, dtype) for shape, dtype in scratch]
        + Plane.scratch() * 6 + Column.scratch() * 12 + Plane.scratch() * 7,
        compiler_params=pltpu.CompilerParams(collective_id=0, has_side_effects=True, vmem_limit_bytes=60 << 20),
        name="whole",
    )(lengths.T, destination.reshape(1, TOK), keys, values, queries, grad_out)
    return settle(*results)


def settle_kernel(*refs):
    sems = refs[8]
    copies = []
    for n in range(4):
        rows = refs[n].shape[0] // 4
        for part in range(4):
            at = pl.ds(part * rows, rows)
            copies.append(pltpu.make_async_copy(refs[n].at[at], refs[4 + n].at[at], sems.at[n, part]))
    for c in copies:
        c.start()
    for c in copies:
        c.wait()


def settle(*results):
    return pl.pallas_call(
        settle_kernel,
        out_shape=tuple(jax.ShapeDtypeStruct(x.shape, x.dtype) for x in results),
        in_specs=[HBM] * 4,
        out_specs=(HBM,) * 4,
        scratch_shapes=[DMA((4, 4))],
        compiler_params=pltpu.CompilerParams(vmem_limit_bytes=60 << 20),
        name="settle",
    )(*results)


def solution(mesh):
    rows = P(("dp", "ctx"), None)
    return jax.shard_map(
        local,
        mesh=mesh,
        in_specs=(rows, rows, rows, rows, P(("dp", "ctx")), P()),
        out_specs=(rows, rows, rows, rows),
        check_vma=False,
    )
```

```python
import functools
import math

import jax
import jax.numpy as jnp
from jax import lax
from jax.experimental import pallas as pl
from jax.experimental.pallas import tpu as pltpu
from jax.sharding import PartitionSpec as P

D = 128
TOK = 192
CAP = 24
F32 = jnp.float32
BF16 = jnp.bfloat16
MESH = pl.DeviceIdType.MESH
VMEM = pl.BlockSpec(memory_space=pltpu.VMEM)
SMEM = pl.BlockSpec(memory_space=pltpu.SMEM)
HBM = pl.BlockSpec(memory_space=pltpu.HBM)
DMA = pltpu.SemaphoreType.DMA
NN = (((1,), (0,)), ((), ()))
NT = (((1,), (1,)), ((), ()))
TN = (((0,), (0,)), ((), ()))
TILE = 256
SCALE = 1.0 / math.sqrt(D)
EXP2 = SCALE * math.log2(math.e)


def dot(a, b, dims=NN):
    return lax.dot_general(a, b, dims, preferred_element_type=F32)


def iota(shape, axis):
    return lax.broadcasted_iota(jnp.int32, shape, axis)


def group_of(dest):
    return ((dest >> 9) * 43) >> 7


def place_of(dest):
    return dest - 192 * (((dest >> 6) * 171) >> 9)


STEPS = [((i + j) % 4, j) for i in range(4) for j in range(4) if (i, j) != (0, 0)]
ROUND = [(1, 0), (3, 0), (2, 0), (1, 1), (3, 1), (2, 1), (0, 1), (0, 0)]


class Here:
    def __init__(self):
        self.dp = lax.axis_index("dp")
        self.ctx = lax.axis_index("ctx")
        self.x, self.y = self.dp // 4, self.dp % 4
        self.z, self.core = self.ctx // 2, self.ctx % 2

    def at(self, dx, dy):
        return ((self.x + (dx + 4) % 4) % 4) * 4 + (self.y + (dy + 4) % 4) % 4

    def chip(self, dz):
        return (self.z + (dz + 4)) % 4

    def peer(self, dz, other):
        return self.chip(dz) * 2 + (self.core + other) % 2


def greet(here):
    barrier = pltpu.get_barrier_semaphore()
    who = [(here.at(*step), here.ctx) for step in STEPS] + [(here.dp, here.peer(*step)) for step in COLUMN[1:]]
    for device in who:
        pl.semaphore_signal(barrier, inc=1, device_id=device, device_id_type=MESH)
    pl.semaphore_wait(barrier, len(who))


def remote(src, dst, send_sem, recv_sem, device):
    return pltpu.make_async_remote_copy(
        src_ref=src, dst_ref=dst, send_sem=send_sem, recv_sem=recv_sem, device_id=device, device_id_type=MESH
    )


class Plane:
    @staticmethod
    def scratch():
        return [DMA((15,)), DMA((15,)), DMA]

    def __init__(self, here, source, target, scratch):
        self.here, self.source, self.target = here, source, target
        self.send_s, self.recv_s, self.own_s = scratch
        self.own = pltpu.make_async_copy(source(here.dp), target(here.dp), self.own_s)
        self.begun = []

    def start_step(self, i):
        to = self.here.at(*STEPS[i])
        c = remote(self.source(to), self.target(self.here.dp), self.send_s.at[i], self.recv_s.at[i], (to, self.here.ctx))
        c.start()
        self.begun.append(c)

    def start(self):
        for i in range(15):
            self.start_step(i)
        self.own.start()

    def finish_in(self):
        for i, (dx, dy) in enumerate(STEPS):
            source = self.here.at(-dx, -dy)
            landing = self.target(source)
            remote(landing, landing, self.send_s.at[i], self.recv_s.at[i], (source, self.here.ctx)).wait_recv()
        self.own.wait()

    def finish_out(self):
        for c in self.begun:
            c.wait_send()


COLUMN = [(0, 0), (0, 1), (1, 0), (1, 1), (3, 0), (3, 1), (2, 0), (2, 1)]


class Column:
    @staticmethod
    def scratch():
        return [DMA((8,)), DMA((8,)), DMA]

    def __init__(self, here, source, target, scratch):
        self.here, self.source, self.target = here, source, target
        self.send_s, self.recv_s, self.own_s = scratch
        self.own = pltpu.make_async_copy(source(here.ctx), target(here.ctx), self.own_s)
        self.begun = []

    def start_to(self, dz, other):
        if (dz, other) == (0, 0):
            self.own.start()
            return
        to, n = self.here.peer(dz, other), 2 * dz + other
        c = remote(self.source(to), self.target(self.here.ctx), self.send_s.at[n], self.recv_s.at[n], (self.here.dp, to))
        c.start()
        self.begun.append(c)

    def start(self):
        for dz, other in ROUND:
            self.start_to(dz, other)

    def finish_chip(self, dz):
        for other in range(2):
            n = 2 * ((4 - dz) % 4) + other
            if n == 0:
                self.own.wait()
                continue
            origin = self.here.peer(dz, other)
            landing = self.target(origin)
            remote(landing, landing, self.send_s.at[n], self.recv_s.at[n], (self.here.dp, origin)).wait_recv()

    def finish_in(self):
        for dz in range(4):
            self.finish_chip(dz)

    def finish_out(self):
        for c in self.begun:
            c.wait_send()


def cols(start, width):
    return pl.ds(pl.multiple_of(start, 128), width)


def rows192(c):
    return pl.ds(pl.multiple_of(192 * c, 64), 192)


def rows48(pair):
    return pl.ds(pl.multiple_of(48 * pair, 16), 48)


def put_in_order(here, exchange, got, opens, hots, slots, out):
    @pl.loop(0, 4)
    def _(i):
        for j in range(4):
            slots[4 * i + j] = dot(opens[4 * i + j], got[4 * i + j]).astype(BF16)

    for dz, other in ROUND:
        pair = here.peer(dz, other)
        x = dot(hots[pair], slots[:, rows48(pair)].reshape(768, D))
        out[pair] = x.astype(BF16).reshape(2, TOK, D)
        exchange.start_to(dz, other)


def put_back(here, exchange, got, backs, hots_t, slots, out):
    @pl.loop(0, 2)
    def _(i):
        for j in range(4):
            pair = 4 * i + j
            x = dot(hots_t[pair], got[pair].reshape(384, D)).astype(BF16)
            slots[:, rows48(pair)] = x.reshape(16, 48, D)

    for i, step in enumerate(STEPS):
        s = here.at(*step)
        out[s] = dot(backs[s], slots[s]).astype(BF16)
        exchange.start_step(i)
    out[here.dp] = dot(backs[here.dp], slots[here.dp]).astype(BF16)
    exchange.own.start()


def tiles():
    for j in range(6):
        low = 0 if j < 4 else 512
        yield j, list(range(low, (j + 1) * TILE, TILE))


def allowed(j, k, end):
    diagonal, mixed = k == j * TILE, j >= 2
    if not diagonal and not mixed:
        return None
    kp = k + iota((TILE, TILE), 0)
    qp = j * TILE + iota((1, TILE), 1)
    mask = None
    if mixed:
        mask = kp >= jnp.where(qp >= end, end, 0)
    if diagonal:
        causal = kp <= qp
        mask = causal if mask is None else mask & causal
    return mask


def forward_unit(e, end, q_ref, k_ref, vt_ref, o_ref, lse_ref):
    for j, ks in tiles():
        rows = slice(j * TILE, j * TILE + TILE)
        q = q_ref[e, rows]
        scores = []
        for k in ks:
            s = dot(k_ref[e, k : k + TILE], q, NT)
            mask = allowed(j, k, end)
            scores.append(s if mask is None else jnp.where(mask, s, -jnp.inf))
        top = jnp.max(functools.reduce(jnp.maximum, scores), axis=0, keepdims=True)
        expo = [jnp.exp2((s - top) * EXP2) for s in scores]
        total = jnp.sum(functools.reduce(jnp.add, expo), axis=0, keepdims=True)
        inverse = 1.0 / total
        att = jnp.zeros((D, TILE), F32)
        for k, x in zip(ks, expo):
            att += dot(vt_ref[e, :, k : k + TILE], (x * inverse).astype(BF16))
        o_ref[e, rows] = jnp.transpose(att).astype(BF16)
        lse_ref[e, :, rows] = top * EXP2 + jnp.log2(total)


def backward_unit(e, end, q_ref, d_ref, o_ref, lse_ref, k_ref, v_ref, kt_ref, gk_ref, gv_ref, gq_ref):
    for j, ks in tiles():
        rows = slice(j * TILE, j * TILE + TILE)
        q, d = q_ref[e, rows], d_ref[e, rows]
        product = d.astype(F32) * o_ref[e, rows].astype(F32)
        delta = jnp.sum(jnp.transpose(product), axis=0, keepdims=True)
        lse = lse_ref[e, :, rows]
        gq = jnp.zeros((D, TILE), F32)
        for k in ks:
            keys = slice(k, k + TILE)
            p = jnp.exp2(dot(k_ref[e, keys], q, NT) * EXP2 - lse)
            mask = allowed(j, k, end)
            if mask is not None:
                p = jnp.where(mask, p, 0.0)
            dp = dot(v_ref[e, keys], d, NT)
            ds = (p * (dp - delta)).astype(BF16)
            gv_ref[e, keys] += dot(p.astype(BF16), d)
            gk_ref[e, keys] += dot(ds, q)
            gq += dot(kt_ref[e, :, keys], ds)
        gq_ref[e, rows] = jnp.transpose(gq * SCALE).astype(BF16)


def whole_kernel(lengths_ref, row_ref, k_ref, v_ref, q_ref, d_ref, oo_ref, oq_ref, ok_ref, ov_ref,
                 info, infos, place, opens, backs, hots, hots_t, slots, got, sent, here_in, here_out, back, ready,
                 kt, vt, lse, gk, gv, parts, *sems):
    here = Here()
    p = here.dp
    sems = [sems[3 * i : 3 * i + 3] for i in range(31)]

    def head_of(ref, h):
        return lambda t: ref.at[:, cols(t * 256 + h * D, D)]

    def kv_head_of(ref):
        return lambda t: ref.at[:, cols((t // 4) * D, D)]

    inward = [kv_head_of(k_ref), kv_head_of(v_ref), head_of(q_ref, 0), head_of(d_ref, 0), head_of(q_ref, 1), head_of(d_ref, 1)]
    p_info = Plane(here, lambda t: info, lambda t: infos.at[t], sems[30])
    p_in = [Plane(here, inward[n], lambda t, n=n: got.at[n, t], sems[n]) for n in range(6)]
    c_in = [Column(here, lambda c, n=n: sent.at[n, c], lambda c, n=n: here_in.at[n, :, rows192(c)], sems[6 + n]) for n in range(6)]
    outward = [head_of(oo_ref, 0), head_of(oq_ref, 0), head_of(oo_ref, 1), head_of(oq_ref, 1)]
    outward += [lambda t: parts.at[0, t], lambda t: parts.at[1, t]]
    c_out = [
        [Column(here, lambda c, n=n, e=e: here_out.at[n, e, rows192(c)], lambda c, n=n, e=e: back.at[n, c, e], sems[6 * e + 12 + n])
         for e in range(2)]
        for n in range(6)
    ]
    p_out = [Plane(here, lambda t, n=n: ready.at[n, t], outward[n], sems[24 + n]) for n in range(6)]

    dest_r = row_ref[...]
    g_r = group_of(dest_r)
    g_c = jnp.transpose(jnp.broadcast_to(g_r.astype(F32), (8, TOK)))[:, 0:1]
    same = (g_r.astype(F32) == g_c) & (iota((TOK, TOK), 0) < iota((TOK, TOK), 1))
    rank = jnp.sum(jnp.where(same, 1.0, 0.0), axis=0, keepdims=True).astype(jnp.int32)
    which = iota((8, TOK), 0)
    info[...] = jnp.where(
        which == 0,
        g_r * CAP + rank,
        jnp.where(which == 1, place_of(dest_r) + 1, jnp.where(which == 2, g_r >> 1, rank + CAP * (g_r & 1))),
    )

    greet(here)
    p_info.start()
    for n in range(3):
        p_in[n].start()

    p_info.finish_in()
    total = jnp.zeros((8, 768), F32)
    for s in range(16):
        opens[s] = jnp.where(iota((384, TOK), 0) == infos[s, 0:1], 1.0, 0.0).astype(BF16)
        named = jnp.where(iota((8, TOK), 0) == infos[s, 2:3], infos[s, 1:2].astype(F32), 0.0).astype(BF16)
        laned = jnp.where(iota((D, TOK), 0) == infos[s, 3:4], 1.0, 0.0).astype(BF16)
        mine = jnp.concatenate([dot(named, laned, NT), jnp.zeros((8, 640), F32)], axis=1)
        total += mine if s == 0 else pltpu.roll(mine, 48 * s, 1)
    odd = (iota((8, 768), 1) % 48) >= CAP
    place[...] = jnp.where(odd & (total > 0.0), total + 192.0, total)

    def hot_of(pair):
        return jnp.where(place[pair : pair + 1] == (iota((384, 768), 0) + 1).astype(F32), 1.0, 0.0)

    for pair in range(8):
        hots[pair] = hot_of(pair).astype(BF16)

    def order(n):
        p_in[n].finish_in()
        if n < 3:
            p_in[n + 3].start()
        put_in_order(here, c_in[n], got.at[n], opens, hots, slots, sent.at[n])

    order(0)
    order(1)
    slot_c = jnp.transpose(jnp.concatenate([infos[s, 0:1].astype(F32) for s in range(16)], axis=0))
    for s in range(16):
        backs[s] = jnp.where(iota((TOK, 384), 1).astype(F32) == slot_c[:, s : s + 1], 1.0, 0.0).astype(BF16)
    order(2)
    place_c = jnp.transpose(place[...])
    for pair in range(8):
        slot_of = (iota((768, 384), 1) + 1).astype(F32) == place_c[:, pair : pair + 1]
        hots_t[pair] = jnp.where(slot_of, 1.0, 0.0).astype(BF16)
    order(3)
    for n, turned in enumerate((kt, vt)):
        c_in[n].finish_in()
        for e in range(2):
            turned[e] = jnp.transpose(here_in[n, e].astype(F32)).astype(BF16)
    gk[...] = jnp.zeros_like(gk)
    gv[...] = jnp.zeros_like(gv)

    def end_of(e):
        return lengths_ref[0, 2 * here.ctx + e]

    def forward(h):
        c_in[2 + 2 * h].finish_in()
        for e in range(2):
            forward_unit(e, end_of(e), here_in.at[2 + 2 * h], here_in.at[0], vt, here_out.at[2 * h], lse.at[h])
            c_out[2 * h][e].start()

    def backward(h, e):
        backward_unit(e, end_of(e), here_in.at[2 + 2 * h], here_in.at[3 + 2 * h], here_out.at[2 * h], lse.at[h],
                      here_in.at[0], here_in.at[1], kt, gk, gv, here_out.at[1 + 2 * h])
        c_out[1 + 2 * h][e].start()
        if h == 1:
            here_out[4, e] = (gk[e] * SCALE).astype(BF16)
            c_out[4][e].start()
            here_out[5, e] = gv[e].astype(BF16)
            c_out[5][e].start()

    def restore(n):
        for c in c_out[n]:
            c.finish_in()
        put_back(here, p_out[n], back.at[n], backs, hots_t, slots, ready.at[n])

    forward(0)
    order(4)
    c_in[3].finish_in()
    backward(0, 0)
    order(5)
    backward(0, 1)
    forward(1)
    restore(0)
    c_in[5].finish_in()
    backward(1, 0)
    restore(1)
    backward(1, 1)
    for n in (2, 3, 4, 5):
        restore(n)
    for n, out in enumerate((ok_ref, ov_ref)):
        p_out[4 + n].finish_in()
        for x in range(4):
            added = parts[n, 4 * x].astype(F32)
            for y in range(1, 4):
                added += parts[n, 4 * x + y].astype(F32)
            out[:, x * D : x * D + D] = added.astype(BF16)
    for x in p_out[:4]:
        x.finish_in()
    for x in [p_info] + p_in + c_in + sum(c_out, []) + p_out:
        x.finish_out()


def local(queries, keys, values, grad_out, destination, lengths):
    scratch = [
        ((8, TOK), jnp.int32), ((16, 8, TOK), jnp.int32), ((8, 768), F32),
        ((16, 384, TOK), BF16), ((16, TOK, 384), BF16), ((8, 384, 768), BF16), ((8, 768, 384), BF16), ((16, 384, D), BF16),
        ((6, 16, TOK, D), BF16), ((6, 8, 2, TOK, D), BF16), ((6, 2, 1536, D), BF16),
        ((6, 2, 1536, D), BF16), ((6, 8, 2, TOK, D), BF16), ((6, 16, TOK, D), BF16),
        ((2, D, 1536), BF16), ((2, D, 1536), BF16), ((2, 2, 1, 1536), F32),
        ((2, 1536, D), F32), ((2, 1536, D), F32), ((2, 16, TOK, D), BF16),
    ]
    results = pl.pallas_call(
        whole_kernel,
        out_shape=(
            jax.ShapeDtypeStruct((TOK, 4096), BF16),
            jax.ShapeDtypeStruct((TOK, 4096), BF16),
            jax.ShapeDtypeStruct((TOK, 512), BF16),
            jax.ShapeDtypeStruct((TOK, 512), BF16),
        ),
        in_specs=[SMEM, VMEM] + [HBM] * 4,
        out_specs=(HBM, HBM, VMEM, VMEM),
        scratch_shapes=[pltpu.VMEM(shape, dtype) for shape, dtype in scratch]
        + Plane.scratch() * 6 + Column.scratch() * 18 + Plane.scratch() * 7,
        compiler_params=pltpu.CompilerParams(collective_id=0, has_side_effects=True, vmem_limit_bytes=60 << 20),
        name="whole",
    )(lengths.T, destination.reshape(1, TOK), keys, values, queries, grad_out)
    return settle(*results)


def settle_kernel(*refs):
    for n in range(4):
        refs[4 + n][...] = refs[n][...]


def settle(*results):
    blocks = [pl.BlockSpec((TOK // 4, x.shape[1]), lambda i: (i, 0)) for x in results]
    return pl.pallas_call(
        settle_kernel,
        out_shape=tuple(jax.ShapeDtypeStruct(x.shape, x.dtype) for x in results),
        grid=(4,),
        in_specs=blocks,
        out_specs=tuple(blocks),
        compiler_params=pltpu.CompilerParams(vmem_limit_bytes=60 << 20),
        name="settle",
    )(*results)


def solution(mesh):
    rows = P(("dp", "ctx"), None)
    return jax.shard_map(
        local,
        mesh=mesh,
        in_specs=(rows, rows, rows, rows, P(("dp", "ctx")), P()),
        out_specs=(rows, rows, rows, rows),
        check_vma=False,
    )
```

```python
import functools
import math

import jax
import jax.numpy as jnp
from jax import lax
from jax.experimental import pallas as pl
from jax.experimental.pallas import tpu as pltpu
from jax.sharding import PartitionSpec as P

D = 128
TOK = 192
CAP = 24
F32 = jnp.float32
BF16 = jnp.bfloat16
MESH = pl.DeviceIdType.MESH
VMEM = pl.BlockSpec(memory_space=pltpu.VMEM)
SMEM = pl.BlockSpec(memory_space=pltpu.SMEM)
HBM = pl.BlockSpec(memory_space=pltpu.HBM)
DMA = pltpu.SemaphoreType.DMA
NN = (((1,), (0,)), ((), ()))
NT = (((1,), (1,)), ((), ()))
TN = (((0,), (0,)), ((), ()))
TILE = 256
SCALE = 1.0 / math.sqrt(D)
EXP2 = SCALE * math.log2(math.e)


def dot(a, b, dims=NN):
    return lax.dot_general(a, b, dims, preferred_element_type=F32)


def iota(shape, axis):
    return lax.broadcasted_iota(jnp.int32, shape, axis)


def group_of(dest):
    return ((dest >> 9) * 43) >> 7


def place_of(dest):
    return dest - 192 * (((dest >> 6) * 171) >> 9)


STEPS = [(1, 0), (-1, 0), (0, 1), (0, -1), (2, 0), (0, 2), (1, 1), (-1, -1), (1, -1), (-1, 1),
         (2, 1), (1, 2), (2, -1), (-1, 2), (2, 2)]
ROUND = [(1, 0), (3, 0), (2, 0), (1, 1), (3, 1), (2, 1), (0, 1), (0, 0)]


class Here:
    def __init__(self):
        self.dp = lax.axis_index("dp")
        self.ctx = lax.axis_index("ctx")
        self.x, self.y = self.dp // 4, self.dp % 4
        self.z, self.core = self.ctx // 2, self.ctx % 2

    def at(self, dx, dy):
        return ((self.x + (dx + 4)) % 4) * 4 + (self.y + (dy + 4)) % 4

    def chip(self, dz):
        return (self.z + (dz + 4)) % 4

    def peer(self, dz, other):
        return self.chip(dz) * 2 + (self.core + other) % 2


def greet(here):
    barrier = pltpu.get_barrier_semaphore()
    who = [(here.at(*step), here.ctx) for step in STEPS] + [(here.dp, here.peer(*step)) for step in COLUMN[1:]]
    for device in who:
        pl.semaphore_signal(barrier, inc=1, device_id=device, device_id_type=MESH)
    pl.semaphore_wait(barrier, len(who))


def remote(src, dst, send_sem, recv_sem, device):
    return pltpu.make_async_remote_copy(
        src_ref=src, dst_ref=dst, send_sem=send_sem, recv_sem=recv_sem, device_id=device, device_id_type=MESH
    )


class Plane:
    @staticmethod
    def scratch():
        return [DMA((15,)), DMA((15,)), DMA]

    def __init__(self, here, source, target, scratch):
        self.here, self.source, self.target = here, source, target
        self.send_s, self.recv_s, self.own_s = scratch
        self.own = pltpu.make_async_copy(source(here.dp), target(here.dp), self.own_s)
        self.begun = []

    def start_step(self, i):
        to = self.here.at(*STEPS[i])
        c = remote(self.source(to), self.target(self.here.dp), self.send_s.at[i], self.recv_s.at[i], (to, self.here.ctx))
        c.start()
        self.begun.append(c)

    def start(self):
        for i in range(15):
            self.start_step(i)
        self.own.start()

    def finish_in(self):
        for i, (dx, dy) in enumerate(STEPS):
            source = self.here.at(-dx, -dy)
            landing = self.target(source)
            remote(landing, landing, self.send_s.at[i], self.recv_s.at[i], (source, self.here.ctx)).wait_recv()
        self.own.wait()

    def finish_out(self):
        for c in self.begun:
            c.wait_send()


COLUMN = [(0, 0), (0, 1), (1, 0), (1, 1), (3, 0), (3, 1), (2, 0), (2, 1)]


class Column:
    @staticmethod
    def scratch():
        return [DMA((8,)), DMA((8,)), DMA]

    def __init__(self, here, source, target, scratch):
        self.here, self.source, self.target = here, source, target
        self.send_s, self.recv_s, self.own_s = scratch
        self.own = pltpu.make_async_copy(source(here.ctx), target(here.ctx), self.own_s)
        self.begun = []

    def start_to(self, dz, other):
        if (dz, other) == (0, 0):
            self.own.start()
            return
        to, n = self.here.peer(dz, other), 2 * dz + other
        c = remote(self.source(to), self.target(self.here.ctx), self.send_s.at[n], self.recv_s.at[n], (self.here.dp, to))
        c.start()
        self.begun.append(c)

    def start(self):
        for dz, other in ROUND:
            self.start_to(dz, other)

    def finish_chip(self, dz):
        for other in range(2):
            n = 2 * ((4 - dz) % 4) + other
            if n == 0:
                self.own.wait()
                continue
            origin = self.here.peer(dz, other)
            landing = self.target(origin)
            remote(landing, landing, self.send_s.at[n], self.recv_s.at[n], (self.here.dp, origin)).wait_recv()

    def finish_in(self):
        for dz in range(4):
            self.finish_chip(dz)

    def finish_out(self):
        for c in self.begun:
            c.wait_send()


def cols(start, width):
    return pl.ds(pl.multiple_of(start, 128), width)


def rows192(c):
    return pl.ds(pl.multiple_of(192 * c, 64), 192)


def rows48(pair):
    return pl.ds(pl.multiple_of(48 * pair, 16), 48)


def put_in_order(here, exchange, got, opens, hots, slots, out):
    for s in range(16):
        slots[s] = dot(opens[s], got[s]).astype(BF16)
    for dz, other in ROUND:
        pair = here.peer(dz, other)
        x = dot(hots[pair], slots[:, rows48(pair)].reshape(768, D))
        out[pair] = x.astype(BF16).reshape(2, TOK, D)
        exchange.start_to(dz, other)


def put_back(here, exchange, got, backs, hots_t, slots, out):
    for pair in range(8):
        x = dot(hots_t[pair], got[pair].reshape(384, D)).astype(BF16)
        slots[:, rows48(pair)] = x.reshape(16, 48, D)
    for i, step in enumerate(STEPS):
        s = here.at(*step)
        out[s] = dot(backs[s], slots[s]).astype(BF16)
        exchange.start_step(i)
    out[here.dp] = dot(backs[here.dp], slots[here.dp]).astype(BF16)
    exchange.own.start()


def tiles():
    for j in range(6):
        low = 0 if j < 4 else 512
        yield j, list(range(low, (j + 1) * TILE, TILE))


def allowed(j, k, end):
    diagonal, mixed = k == j * TILE, j >= 2 and k < 1024
    if not diagonal and not mixed:
        return None
    kp = k + iota((TILE, TILE), 0)
    qp = j * TILE + iota((1, TILE), 1)
    mask = None
    if mixed:
        mask = kp >= jnp.where(qp >= end, end, 0)
    if diagonal:
        causal = kp <= qp
        mask = causal if mask is None else mask & causal
    return mask


def forward_unit(e, end, q_ref, k_ref, vt_ref, o_ref, lse_ref):
    for j, ks in tiles():
        rows = slice(j * TILE, j * TILE + TILE)
        q = q_ref[e, rows]
        scores = []
        for k in ks:
            s = dot(k_ref[e, k : k + TILE], q, NT)
            mask = allowed(j, k, end)
            scores.append(s if mask is None else jnp.where(mask, s, -jnp.inf))
        top = jnp.max(functools.reduce(jnp.maximum, scores), axis=0, keepdims=True)
        expo = [jnp.exp2((s - top) * EXP2) for s in scores]
        total = jnp.sum(functools.reduce(jnp.add, expo), axis=0, keepdims=True)
        inverse = 1.0 / total
        att = jnp.zeros((D, TILE), F32)
        for k, x in zip(ks, expo):
            att += dot(vt_ref[e, :, k : k + TILE], (x * inverse).astype(BF16))
        o_ref[e, rows] = jnp.transpose(att).astype(BF16)
        lse_ref[e, :, rows] = top * EXP2 + jnp.log2(total)


def backward_unit(e, end, q_ref, d_ref, o_ref, lse_ref, k_ref, v_ref, kt_ref, gk_ref, gv_ref, gq_ref):
    for j, ks in tiles():
        rows = slice(j * TILE, j * TILE + TILE)
        q, d = q_ref[e, rows], d_ref[e, rows]
        product = d.astype(F32) * o_ref[e, rows].astype(F32)
        delta = jnp.sum(jnp.transpose(product), axis=0, keepdims=True)
        lse = lse_ref[e, :, rows]
        gq = jnp.zeros((D, TILE), F32)
        for k in ks:
            keys = slice(k, k + TILE)
            p = jnp.exp2(dot(k_ref[e, keys], q, NT) * EXP2 - lse)
            mask = allowed(j, k, end)
            if mask is not None:
                p = jnp.where(mask, p, 0.0)
            dp = dot(v_ref[e, keys], d, NT)
            ds = (p * (dp - delta)).astype(BF16)
            gv_ref[e, keys] += dot(p.astype(BF16), d)
            gk_ref[e, keys] += dot(ds, q)
            gq += dot(kt_ref[e, :, keys], ds)
        gq_ref[e, rows] = jnp.transpose(gq * SCALE).astype(BF16)


def whole_kernel(lengths_ref, row_ref, k_ref, v_ref, q_ref, d_ref, oo_ref, oq_ref, ok_ref, ov_ref,
                 info, infos, place, opens, backs, hots, hots_t, slots, got, sent, here_in, here_out, back, ready,
                 kt, vt, lse, gk, gv, parts, *sems):
    here = Here()
    p = here.dp
    sems = [sems[3 * i : 3 * i + 3] for i in range(25)]

    def head_of(ref, h):
        return lambda t: ref.at[:, cols(t * 256 + h * D, D)]

    def kv_head_of(ref):
        return lambda t: ref.at[:, cols((t // 4) * D, D)]

    inward = [kv_head_of(k_ref), kv_head_of(v_ref), head_of(q_ref, 0), head_of(d_ref, 0), head_of(q_ref, 1), head_of(d_ref, 1)]
    p_info = Plane(here, lambda t: info, lambda t: infos.at[t], sems[24])
    p_in = [Plane(here, inward[n], lambda t, n=n: got.at[n, t], sems[n]) for n in range(6)]
    c_in = [Column(here, lambda c, n=n: sent.at[n, c], lambda c, n=n: here_in.at[n, :, rows192(c)], sems[6 + n]) for n in range(6)]
    outward = [head_of(oo_ref, 0), head_of(oq_ref, 0), head_of(oo_ref, 1), head_of(oq_ref, 1)]
    outward += [lambda t: parts.at[0, t], lambda t: parts.at[1, t]]
    c_out = [Column(here, lambda c, n=n: here_out.at[n, :, rows192(c)], lambda c, n=n: back.at[n, c], sems[12 + n]) for n in range(6)]
    p_out = [Plane(here, lambda t, n=n: ready.at[n, t], outward[n], sems[18 + n]) for n in range(6)]

    dest_r = row_ref[...]
    g_r = group_of(dest_r)
    g_c = jnp.transpose(jnp.broadcast_to(g_r.astype(F32), (8, TOK)))[:, 0:1]
    same = (g_r.astype(F32) == g_c) & (iota((TOK, TOK), 0) < iota((TOK, TOK), 1))
    rank = jnp.sum(jnp.where(same, 1.0, 0.0), axis=0, keepdims=True).astype(jnp.int32)
    which = iota((8, TOK), 0)
    info[...] = jnp.where(
        which == 0,
        g_r * CAP + rank,
        jnp.where(which == 1, place_of(dest_r) + 1, jnp.where(which == 2, g_r >> 1, rank + CAP * (g_r & 1))),
    )

    greet(here)
    p_info.start()
    for n in range(3):
        p_in[n].start()

    p_info.finish_in()
    total = jnp.zeros((8, 768), F32)
    for s in range(16):
        opens[s] = jnp.where(iota((384, TOK), 0) == infos[s, 0:1], 1.0, 0.0).astype(BF16)
        named = jnp.where(iota((8, TOK), 0) == infos[s, 2:3], infos[s, 1:2].astype(F32), 0.0).astype(BF16)
        laned = jnp.where(iota((D, TOK), 0) == infos[s, 3:4], 1.0, 0.0).astype(BF16)
        mine = jnp.concatenate([dot(named, laned, NT), jnp.zeros((8, 640), F32)], axis=1)
        total += mine if s == 0 else pltpu.roll(mine, 48 * s, 1)
    odd = (iota((8, 768), 1) % 48) >= CAP
    place[...] = jnp.where(odd & (total > 0.0), total + 192.0, total)

    def hot_of(pair):
        return jnp.where(place[pair : pair + 1] == (iota((384, 768), 0) + 1).astype(F32), 1.0, 0.0)

    for pair in range(8):
        hots[pair] = hot_of(pair).astype(BF16)

    def order(n):
        p_in[n].finish_in()
        if n < 3:
            p_in[n + 3].start()
        put_in_order(here, c_in[n], got.at[n], opens, hots, slots, sent.at[n])

    order(0)
    order(1)
    slot_c = jnp.transpose(jnp.concatenate([infos[s, 0:1].astype(F32) for s in range(16)], axis=0))
    for s in range(16):
        backs[s] = jnp.where(iota((TOK, 384), 1).astype(F32) == slot_c[:, s : s + 1], 1.0, 0.0).astype(BF16)
    order(2)
    place_c = jnp.transpose(place[...])
    for pair in range(8):
        slot_of = (iota((768, 384), 1) + 1).astype(F32) == place_c[:, pair : pair + 1]
        hots_t[pair] = jnp.where(slot_of, 1.0, 0.0).astype(BF16)
    order(3)
    for n, turned in enumerate((kt, vt)):
        c_in[n].finish_in()
        for e in range(2):
            turned[e] = jnp.transpose(here_in[n, e].astype(F32)).astype(BF16)
    gk[...] = jnp.zeros_like(gk)
    gv[...] = jnp.zeros_like(gv)

    def end_of(e):
        return lengths_ref[0, 2 * here.ctx + e]

    def forward(h):
        c_in[2 + 2 * h].finish_in()

        @pl.loop(0, 2)
        def _(e):
            forward_unit(e, end_of(e), here_in.at[2 + 2 * h], here_in.at[0], vt, here_out.at[2 * h], lse.at[h])

        c_out[2 * h].start()

    def backward(h, e):
        backward_unit(e, end_of(e), here_in.at[2 + 2 * h], here_in.at[3 + 2 * h], here_out.at[2 * h], lse.at[h],
                      here_in.at[0], here_in.at[1], kt, gk, gv, here_out.at[1 + 2 * h])

    def restore(n):
        c_out[n].finish_in()
        put_back(here, p_out[n], back.at[n], backs, hots_t, slots, ready.at[n])

    forward(0)
    order(4)
    c_in[3].finish_in()
    backward(0, 0)
    order(5)
    backward(0, 1)
    c_out[1].start()
    restore(0)
    forward(1)
    c_in[5].finish_in()
    backward(1, 0)
    restore(1)
    backward(1, 1)
    c_out[3].start()
    here_out[4] = (gk[...] * SCALE).astype(BF16)
    c_out[4].start()
    here_out[5] = gv[...].astype(BF16)
    c_out[5].start()
    for n in (2, 3, 4, 5):
        restore(n)
    for x in [p_info] + p_in + c_in + c_out + p_out[:4]:
        x.finish_out()
    for x in p_out[:4]:
        x.finish_in()
    for n, out in enumerate((ok_ref, ov_ref)):
        p_out[4 + n].finish_in()
        for x in range(4):
            added = parts[n, 4 * x].astype(F32)
            for y in range(1, 4):
                added += parts[n, 4 * x + y].astype(F32)
            out[:, x * D : x * D + D] = added.astype(BF16)
    for x in p_out[4:]:
        x.finish_out()


def local(queries, keys, values, grad_out, destination, lengths):
    scratch = [
        ((8, TOK), jnp.int32), ((16, 8, TOK), jnp.int32), ((8, 768), F32),
        ((16, 384, TOK), BF16), ((16, TOK, 384), BF16), ((8, 384, 768), BF16), ((8, 768, 384), BF16), ((16, 384, D), BF16),
        ((6, 16, TOK, D), BF16), ((6, 8, 2, TOK, D), BF16), ((6, 2, 1536, D), BF16),
        ((6, 2, 1536, D), BF16), ((6, 8, 2, TOK, D), BF16), ((6, 16, TOK, D), BF16),
        ((2, D, 1536), BF16), ((2, D, 1536), BF16), ((2, 2, 1, 1536), F32),
        ((2, 1536, D), F32), ((2, 1536, D), F32), ((2, 16, TOK, D), BF16),
    ]
    results = pl.pallas_call(
        whole_kernel,
        out_shape=(
            jax.ShapeDtypeStruct((TOK, 4096), BF16),
            jax.ShapeDtypeStruct((TOK, 4096), BF16),
            jax.ShapeDtypeStruct((TOK, 512), BF16),
            jax.ShapeDtypeStruct((TOK, 512), BF16),
        ),
        in_specs=[SMEM, VMEM] + [HBM] * 4,
        out_specs=(HBM, HBM, VMEM, VMEM),
        scratch_shapes=[pltpu.VMEM(shape, dtype) for shape, dtype in scratch]
        + Plane.scratch() * 6 + Column.scratch() * 12 + Plane.scratch() * 7,
        compiler_params=pltpu.CompilerParams(collective_id=0, has_side_effects=True, vmem_limit_bytes=60 << 20),
        name="whole",
    )(lengths.T, destination.reshape(1, TOK), keys, values, queries, grad_out)
    return settle(*results)


def settle_kernel(*refs):
    for n in range(4):
        refs[4 + n][...] = refs[n][...]


def settle(*results):
    blocks = [pl.BlockSpec((TOK // 4, x.shape[1]), lambda i: (i, 0)) for x in results]
    return pl.pallas_call(
        settle_kernel,
        out_shape=tuple(jax.ShapeDtypeStruct(x.shape, x.dtype) for x in results),
        grid=(4,),
        in_specs=blocks,
        out_specs=tuple(blocks),
        compiler_params=pltpu.CompilerParams(vmem_limit_bytes=60 << 20),
        name="settle",
    )(*results)


def solution(mesh):
    rows = P(("dp", "ctx"), None)
    return jax.shard_map(
        local,
        mesh=mesh,
        in_specs=(rows, rows, rows, rows, P(("dp", "ctx")), P()),
        out_specs=(rows, rows, rows, rows),
        check_vma=False,
    )
```

```python
import functools
import math

import jax
import jax.numpy as jnp
from jax import lax
from jax.experimental import pallas as pl
from jax.experimental.pallas import tpu as pltpu
from jax.sharding import PartitionSpec as P

D = 128
TOK = 192
CAP = 24
F32 = jnp.float32
BF16 = jnp.bfloat16
MESH = pl.DeviceIdType.MESH
VMEM = pl.BlockSpec(memory_space=pltpu.VMEM)
SMEM = pl.BlockSpec(memory_space=pltpu.SMEM)
HBM = pl.BlockSpec(memory_space=pltpu.HBM)
DMA = pltpu.SemaphoreType.DMA
NN = (((1,), (0,)), ((), ()))
NT = (((1,), (1,)), ((), ()))
TN = (((0,), (0,)), ((), ()))
TILE = 256
SCALE = 1.0 / math.sqrt(D)
EXP2 = SCALE * math.log2(math.e)


def dot(a, b, dims=NN):
    return lax.dot_general(a, b, dims, preferred_element_type=F32)


def iota(shape, axis):
    return lax.broadcasted_iota(jnp.int32, shape, axis)


def group_of(dest):
    return ((dest >> 9) * 43) >> 7


def place_of(dest):
    return dest - 192 * (((dest >> 6) * 171) >> 9)


STEPS = [(1, 0), (-1, 0), (0, 1), (0, -1), (2, 0), (0, 2), (1, 1), (-1, -1), (1, -1), (-1, 1),
         (2, 1), (1, 2), (2, -1), (-1, 2), (2, 2)]
ROUND = [(1, 0), (3, 0), (2, 0), (1, 1), (3, 1), (2, 1), (0, 1), (0, 0)]


class Here:
    def __init__(self):
        self.dp = lax.axis_index("dp")
        self.ctx = lax.axis_index("ctx")
        self.x, self.y = self.dp // 4, self.dp % 4
        self.z, self.core = self.ctx // 2, self.ctx % 2

    def at(self, dx, dy):
        return ((self.x + (dx + 4)) % 4) * 4 + (self.y + (dy + 4)) % 4

    def chip(self, dz):
        return (self.z + (dz + 4)) % 4

    def peer(self, dz, other):
        return self.chip(dz) * 2 + (self.core + other) % 2


def greet(here):
    barrier = pltpu.get_barrier_semaphore()
    who = [(here.at(*step), here.ctx) for step in STEPS] + [(here.dp, here.peer(*step)) for step in COLUMN[1:]]
    for device in who:
        pl.semaphore_signal(barrier, inc=1, device_id=device, device_id_type=MESH)
    pl.semaphore_wait(barrier, len(who))


def remote(src, dst, send_sem, recv_sem, device):
    return pltpu.make_async_remote_copy(
        src_ref=src, dst_ref=dst, send_sem=send_sem, recv_sem=recv_sem, device_id=device, device_id_type=MESH
    )


class Plane:
    def __init__(self, here, source, target, span, scratch):
        self.here, self.source, self.target = here, source, target
        self.send_s, self.recv_s, self.own_s = scratch
        self.own = pltpu.make_async_copy(source(here.dp), target(here.dp), self.own_s)
        self.all = remote(span, span, self.send_s, self.recv_s, (here.at(1, 0), here.ctx))

    def start_step(self, i):
        to = self.here.at(*STEPS[i])
        remote(self.source(to), self.target(self.here.dp), self.send_s, self.recv_s, (to, self.here.ctx)).start()

    def start(self):
        for i in range(15):
            self.start_step(i)
        self.own.start()

    def finish_in(self):
        self.all.wait_recv()
        self.own.wait()

    def finish_out(self):
        self.all.wait_send()


COLUMN = [(0, 0), (0, 1), (1, 0), (1, 1), (3, 0), (3, 1), (2, 0), (2, 1)]


class Column:
    def __init__(self, here, source, target, span, scratch):
        self.here, self.source, self.target = here, source, target
        self.send_s, self.recv_s, self.own_s = scratch
        self.own = pltpu.make_async_copy(source(here.ctx), target(here.ctx), self.own_s)
        self.all = remote(span, span, self.send_s, self.recv_s, (here.dp, here.peer(0, 1)))

    def start_to(self, dz, other):
        if (dz, other) == (0, 0):
            self.own.start()
            return
        to = self.here.peer(dz, other)
        remote(self.source(to), self.target(self.here.ctx), self.send_s, self.recv_s, (self.here.dp, to)).start()

    def start(self):
        for dz, other in ROUND:
            self.start_to(dz, other)

    def finish_in(self):
        self.all.wait_recv()
        self.own.wait()

    def finish_out(self):
        self.all.wait_send()


def cols(start, width):
    return pl.ds(pl.multiple_of(start, 128), width)


def rows192(c):
    return pl.ds(pl.multiple_of(192 * c, 64), 192)


def rows48(pair):
    return pl.ds(pl.multiple_of(48 * pair, 16), 48)


def put_in_order(here, exchange, got, opens, hots, slots, out):
    for s in range(16):
        slots[s] = dot(opens[s], got[s]).astype(BF16)
    for dz, other in ROUND:
        pair = here.peer(dz, other)
        x = dot(hots[pair], slots[:, rows48(pair)].reshape(768, D))
        out[pair] = x.astype(BF16).reshape(2, TOK, D)
        exchange.start_to(dz, other)


def put_back(here, exchange, got, backs, hots_t, slots, out):
    for pair in range(8):
        x = dot(hots_t[pair], got[pair].reshape(384, D)).astype(BF16)
        slots[:, rows48(pair)] = x.reshape(16, 48, D)
    for i, step in enumerate(STEPS):
        s = here.at(*step)
        out[s] = dot(backs[s], slots[s]).astype(BF16)
        exchange.start_step(i)
    out[here.dp] = dot(backs[here.dp], slots[here.dp]).astype(BF16)
    exchange.own.start()


def tiles():
    for j in range(6):
        low = 0 if j < 4 else 512
        yield j, list(range(low, (j + 1) * TILE, TILE))


def allowed(j, k, end):
    diagonal, mixed = k == j * TILE, j >= 2 and k < 1024
    if not diagonal and not mixed:
        return None
    kp = k + iota((TILE, TILE), 0)
    qp = j * TILE + iota((1, TILE), 1)
    mask = None
    if mixed:
        mask = kp >= jnp.where(qp >= end, end, 0)
    if diagonal:
        causal = kp <= qp
        mask = causal if mask is None else mask & causal
    return mask


def forward_unit(e, end, q_ref, k_ref, vt_ref, o_ref, lse_ref):
    for j, ks in tiles():
        rows = slice(j * TILE, j * TILE + TILE)
        q = q_ref[e, rows]
        scores = []
        for k in ks:
            s = dot(k_ref[e, k : k + TILE], q, NT)
            mask = allowed(j, k, end)
            scores.append(s if mask is None else jnp.where(mask, s, -jnp.inf))
        top = jnp.max(functools.reduce(jnp.maximum, scores), axis=0, keepdims=True)
        expo = [jnp.exp2((s - top) * EXP2) for s in scores]
        total = jnp.sum(functools.reduce(jnp.add, expo), axis=0, keepdims=True)
        inverse = 1.0 / total
        att = jnp.zeros((D, TILE), F32)
        for k, x in zip(ks, expo):
            att += dot(vt_ref[e, :, k : k + TILE], (x * inverse).astype(BF16))
        o_ref[e, rows] = jnp.transpose(att).astype(BF16)
        lse_ref[e, :, rows] = top * EXP2 + jnp.log2(total)


def backward_unit(e, end, q_ref, d_ref, o_ref, lse_ref, k_ref, v_ref, kt_ref, gk_ref, gv_ref, gq_ref):
    for j, ks in tiles():
        rows = slice(j * TILE, j * TILE + TILE)
        q, d = q_ref[e, rows], d_ref[e, rows]
        product = d.astype(F32) * o_ref[e, rows].astype(F32)
        delta = jnp.sum(jnp.transpose(product), axis=0, keepdims=True)
        lse = lse_ref[e, :, rows]
        gq = jnp.zeros((D, TILE), F32)
        for k in ks:
            keys = slice(k, k + TILE)
            p = jnp.exp2(dot(k_ref[e, keys], q, NT) * EXP2 - lse)
            mask = allowed(j, k, end)
            if mask is not None:
                p = jnp.where(mask, p, 0.0)
            dp = dot(v_ref[e, keys], d, NT)
            ds = (p * (dp - delta)).astype(BF16)
            gv_ref[e, keys] += dot(p.astype(BF16), d)
            gk_ref[e, keys] += dot(ds, q)
            gq += dot(kt_ref[e, :, keys], ds)
        gq_ref[e, rows] = jnp.transpose(gq * SCALE).astype(BF16)


def whole_kernel(lengths_ref, row_ref, k_ref, v_ref, q_ref, d_ref, oo_ref, oq_ref, ok_ref, ov_ref,
                 info, infos, place, opens, backs, hots, hots_t, slots, got, sent, here_in, here_out, back, ready,
                 kt, vt, lse, gk, gv, parts, *sems):
    here = Here()
    p = here.dp
    sems = [sems[3 * i : 3 * i + 3] for i in range(25)]

    def head_of(ref, h):
        return lambda t: ref.at[:, cols(t * 256 + h * D, D)]

    def kv_head_of(ref):
        return lambda t: ref.at[:, cols((t // 4) * D, D)]

    inward = [kv_head_of(k_ref), kv_head_of(v_ref), head_of(q_ref, 0), head_of(d_ref, 0), head_of(q_ref, 1), head_of(d_ref, 1)]
    p_info = Plane(here, lambda t: info, lambda t: infos.at[t], infos.at[pl.ds(0, 15)], sems[24])
    p_in = [Plane(here, inward[n], lambda t, n=n: got.at[n, t], got.at[n, pl.ds(0, 15)], sems[n]) for n in range(6)]
    c_in = [
        Column(here, lambda c, n=n: sent.at[n, c], lambda c, n=n: here_in.at[n, :, rows192(c)],
               here_in.at[n, :, pl.ds(0, 7 * TOK)], sems[6 + n])
        for n in range(6)
    ]
    outward = [head_of(oo_ref, 0), head_of(oq_ref, 0), head_of(oo_ref, 1), head_of(oq_ref, 1)]
    outward += [lambda t: parts.at[0, t], lambda t: parts.at[1, t]]
    c_out = [
        Column(here, lambda c, n=n: here_out.at[n, :, rows192(c)], lambda c, n=n: back.at[n, c],
               back.at[n, pl.ds(0, 7)], sems[12 + n])
        for n in range(6)
    ]
    spans = [ref.at[:, pl.ds(0, 15 * D)] for ref in (oo_ref, oq_ref, oo_ref, oq_ref)]
    spans += [parts.at[n, pl.ds(0, 15)] for n in range(2)]
    p_out = [Plane(here, lambda t, n=n: ready.at[n, t], outward[n], spans[n], sems[18 + n]) for n in range(6)]

    greet(here)
    p_in[0].start()
    dest_r = row_ref[...]
    g_r = group_of(dest_r)
    g_c = jnp.transpose(jnp.broadcast_to(g_r.astype(F32), (8, TOK)))[:, 0:1]
    same = (g_r.astype(F32) == g_c) & (iota((TOK, TOK), 0) < iota((TOK, TOK), 1))
    rank = jnp.sum(jnp.where(same, 1.0, 0.0), axis=0, keepdims=True).astype(jnp.int32)
    which = iota((8, TOK), 0)
    info[...] = jnp.where(
        which == 0,
        g_r * CAP + rank,
        jnp.where(which == 1, place_of(dest_r) + 1, jnp.where(which == 2, g_r >> 1, rank + CAP * (g_r & 1))),
    )

    p_info.start()
    p_in[1].start()
    p_in[2].start()

    p_info.finish_in()
    total = jnp.zeros((8, 768), F32)
    for s in range(16):
        opens[s] = jnp.where(iota((384, TOK), 0) == infos[s, 0:1], 1.0, 0.0).astype(BF16)
        named = jnp.where(iota((8, TOK), 0) == infos[s, 2:3], infos[s, 1:2].astype(F32), 0.0).astype(BF16)
        laned = jnp.where(iota((D, TOK), 0) == infos[s, 3:4], 1.0, 0.0).astype(BF16)
        mine = jnp.concatenate([dot(named, laned, NT), jnp.zeros((8, 640), F32)], axis=1)
        total += mine if s == 0 else pltpu.roll(mine, 48 * s, 1)
    odd = (iota((8, 768), 1) % 48) >= CAP
    place[...] = jnp.where(odd & (total > 0.0), total + 192.0, total)

    def hot_of(pair):
        return jnp.where(place[pair : pair + 1] == (iota((384, 768), 0) + 1).astype(F32), 1.0, 0.0)

    for pair in range(8):
        hots[pair] = hot_of(pair).astype(BF16)

    def order(n):
        p_in[n].finish_in()
        if n < 3:
            p_in[n + 3].start()
        put_in_order(here, c_in[n], got.at[n], opens, hots, slots, sent.at[n])

    order(0)
    order(1)
    slot_c = jnp.transpose(jnp.concatenate([infos[s, 0:1].astype(F32) for s in range(16)], axis=0))
    for s in range(16):
        backs[s] = jnp.where(iota((TOK, 384), 1).astype(F32) == slot_c[:, s : s + 1], 1.0, 0.0).astype(BF16)
    order(2)
    place_c = jnp.transpose(place[...])
    for pair in range(8):
        slot_of = (iota((768, 384), 1) + 1).astype(F32) == place_c[:, pair : pair + 1]
        hots_t[pair] = jnp.where(slot_of, 1.0, 0.0).astype(BF16)
    order(3)
    for n, turned in enumerate((kt, vt)):
        c_in[n].finish_in()
        for e in range(2):
            turned[e] = jnp.transpose(here_in[n, e].astype(F32)).astype(BF16)
    gk[...] = jnp.zeros_like(gk)
    gv[...] = jnp.zeros_like(gv)

    def end_of(e):
        return lengths_ref[0, 2 * here.ctx + e]

    def forward(h):
        c_in[2 + 2 * h].finish_in()

        @pl.loop(0, 2)
        def _(e):
            forward_unit(e, end_of(e), here_in.at[2 + 2 * h], here_in.at[0], vt, here_out.at[2 * h], lse.at[h])

        c_out[2 * h].start()

    def backward(h, e):
        backward_unit(e, end_of(e), here_in.at[2 + 2 * h], here_in.at[3 + 2 * h], here_out.at[2 * h], lse.at[h],
                      here_in.at[0], here_in.at[1], kt, gk, gv, here_out.at[1 + 2 * h])

    def restore(n):
        c_out[n].finish_in()
        put_back(here, p_out[n], back.at[n], backs, hots_t, slots, ready.at[n])

    forward(0)
    order(4)
    c_in[3].finish_in()
    backward(0, 0)
    order(5)
    backward(0, 1)
    c_out[1].start()
    restore(0)
    forward(1)
    c_in[5].finish_in()
    backward(1, 0)
    restore(1)
    backward(1, 1)
    c_out[3].start()
    here_out[4] = (gk[...] * SCALE).astype(BF16)
    c_out[4].start()
    here_out[5] = gv[...].astype(BF16)
    c_out[5].start()
    for n in (2, 3, 4, 5):
        restore(n)
    for x in [p_info] + p_in + c_in + c_out + p_out[:4]:
        x.finish_out()
    for x in p_out[:4]:
        x.finish_in()
    for n, out in enumerate((ok_ref, ov_ref)):
        p_out[4 + n].finish_in()
        for x in range(4):
            added = parts[n, 4 * x].astype(F32)
            for y in range(1, 4):
                added += parts[n, 4 * x + y].astype(F32)
            out[:, x * D : x * D + D] = added.astype(BF16)
    for x in p_out[4:]:
        x.finish_out()


def local(queries, keys, values, grad_out, destination, lengths):
    scratch = [
        ((8, TOK), jnp.int32), ((16, 8, TOK), jnp.int32), ((8, 768), F32),
        ((16, 384, TOK), BF16), ((16, TOK, 384), BF16), ((8, 384, 768), BF16), ((8, 768, 384), BF16), ((16, 384, D), BF16),
        ((6, 16, TOK, D), BF16), ((6, 8, 2, TOK, D), BF16), ((6, 2, 1536, D), BF16),
        ((6, 2, 1536, D), BF16), ((6, 8, 2, TOK, D), BF16), ((6, 16, TOK, D), BF16),
        ((2, D, 1536), BF16), ((2, D, 1536), BF16), ((2, 2, 1, 1536), F32),
        ((2, 1536, D), F32), ((2, 1536, D), F32), ((2, 16, TOK, D), BF16),
    ]
    results = pl.pallas_call(
        whole_kernel,
        out_shape=(
            jax.ShapeDtypeStruct((TOK, 4096), BF16),
            jax.ShapeDtypeStruct((TOK, 4096), BF16),
            jax.ShapeDtypeStruct((TOK, 512), BF16),
            jax.ShapeDtypeStruct((TOK, 512), BF16),
        ),
        in_specs=[SMEM, VMEM] + [HBM] * 4,
        out_specs=(HBM, HBM, VMEM, VMEM),
        scratch_shapes=[pltpu.VMEM(shape, dtype) for shape, dtype in scratch]
        + [DMA] * 75,
        compiler_params=pltpu.CompilerParams(collective_id=0, has_side_effects=True, vmem_limit_bytes=60 << 20),
        name="whole",
    )(lengths.T, destination.reshape(1, TOK), keys, values, queries, grad_out)
    return settle(*results)


def settle_kernel(*refs):
    ins, outs, held, (load, store) = refs[:4], refs[4:8], refs[8:12], refs[12:]
    parts = [(n, part) for n in range(4) for part in range(4)]
    loads, stores = [], []
    for n, part in parts:
        rows = pl.ds(part * (TOK // 4), TOK // 4)
        loads.append(pltpu.make_async_copy(ins[n].at[rows], held[n].at[rows], load.at[n, part]))
        stores.append(pltpu.make_async_copy(held[n].at[rows], outs[n].at[rows], store.at[n, part]))
    for c in loads:
        c.start()
    for first, second in zip(loads, stores):
        first.wait()
        second.start()
    for c in stores:
        c.wait()


def settle(*results):
    return pl.pallas_call(
        settle_kernel,
        out_shape=tuple(jax.ShapeDtypeStruct(x.shape, x.dtype) for x in results),
        in_specs=[HBM] * 4,
        out_specs=(HBM,) * 4,
        scratch_shapes=[pltpu.VMEM(x.shape, x.dtype) for x in results] + [DMA((4, 4)), DMA((4, 4))],
        compiler_params=pltpu.CompilerParams(vmem_limit_bytes=60 << 20),
        name="settle",
    )(*results)


def solution(mesh):
    rows = P(("dp", "ctx"), None)
    return jax.shard_map(
        local,
        mesh=mesh,
        in_specs=(rows, rows, rows, rows, P(("dp", "ctx")), P()),
        out_specs=(rows, rows, rows, rows),
        check_vma=False,
    )
```

```python
import functools
import math

import jax
import jax.numpy as jnp
from jax import lax
from jax.experimental import pallas as pl
from jax.experimental.pallas import tpu as pltpu
from jax.sharding import PartitionSpec as P

D = 128
TOK = 192
CAP = 24
F32 = jnp.float32
BF16 = jnp.bfloat16
MESH = pl.DeviceIdType.MESH
VMEM = pl.BlockSpec(memory_space=pltpu.VMEM)
SMEM = pl.BlockSpec(memory_space=pltpu.SMEM)
HBM = pl.BlockSpec(memory_space=pltpu.HBM)
DMA = pltpu.SemaphoreType.DMA
NN = (((1,), (0,)), ((), ()))
NT = (((1,), (1,)), ((), ()))
TN = (((0,), (0,)), ((), ()))
TILE = 256
SCALE = 1.0 / math.sqrt(D)
EXP2 = SCALE * math.log2(math.e)


def dot(a, b, dims=NN):
    return lax.dot_general(a, b, dims, preferred_element_type=F32)


def iota(shape, axis):
    return lax.broadcasted_iota(jnp.int32, shape, axis)


def group_of(dest):
    return ((dest >> 9) * 43) >> 7


def place_of(dest):
    return dest - 192 * (((dest >> 6) * 171) >> 9)


STEPS = [(1, 0), (-1, 0), (0, 1), (0, -1), (2, 0), (0, 2), (1, 1), (-1, -1), (1, -1), (-1, 1),
         (2, 1), (1, 2), (2, -1), (-1, 2), (2, 2)]
ROUND = [(1, 0), (3, 0), (2, 0), (1, 1), (3, 1), (2, 1), (0, 1), (0, 0)]


class Here:
    def __init__(self):
        self.dp = lax.axis_index("dp")
        self.ctx = lax.axis_index("ctx")
        self.x, self.y = self.dp // 4, self.dp % 4
        self.z, self.core = self.ctx // 2, self.ctx % 2

    def at(self, dx, dy):
        return ((self.x + (dx + 4)) % 4) * 4 + (self.y + (dy + 4)) % 4

    def chip(self, dz):
        return (self.z + (dz + 4)) % 4

    def peer(self, dz, other):
        return self.chip(dz) * 2 + (self.core + other) % 2


def greet(here):
    barrier = pltpu.get_barrier_semaphore()
    who = [(here.at(*step), here.ctx) for step in STEPS] + [(here.dp, here.peer(*step)) for step in COLUMN[1:]]
    for device in who:
        pl.semaphore_signal(barrier, inc=1, device_id=device, device_id_type=MESH)
    pl.semaphore_wait(barrier, len(who))


def remote(src, dst, send_sem, recv_sem, device):
    return pltpu.make_async_remote_copy(
        src_ref=src, dst_ref=dst, send_sem=send_sem, recv_sem=recv_sem, device_id=device, device_id_type=MESH
    )


class Plane:
    def __init__(self, here, source, target, span, scratch):
        self.here, self.source, self.target = here, source, target
        self.send_s, self.recv_s, self.own_s = scratch
        self.own = pltpu.make_async_copy(source(here.dp), target(here.dp), self.own_s)
        self.all = remote(span, span, self.send_s, self.recv_s, (here.at(1, 0), here.ctx))

    def start_step(self, i):
        to = self.here.at(*STEPS[i])
        remote(self.source(to), self.target(self.here.dp), self.send_s, self.recv_s, (to, self.here.ctx)).start()

    def start(self):
        for i in range(15):
            self.start_step(i)
        self.own.start()

    def finish_in(self):
        self.all.wait_recv()
        self.own.wait()

    def finish_out(self):
        self.all.wait_send()


COLUMN = [(0, 0), (0, 1), (1, 0), (1, 1), (3, 0), (3, 1), (2, 0), (2, 1)]


class Column:
    def __init__(self, here, source, target, span, scratch):
        self.here, self.source, self.target = here, source, target
        self.send_s, self.recv_s, self.own_s = scratch
        self.own = pltpu.make_async_copy(source(here.ctx), target(here.ctx), self.own_s)
        self.all = remote(span, span, self.send_s, self.recv_s, (here.dp, here.peer(0, 1)))

    def start_to(self, dz, other):
        if (dz, other) == (0, 0):
            self.own.start()
            return
        to = self.here.peer(dz, other)
        remote(self.source(to), self.target(self.here.ctx), self.send_s, self.recv_s, (self.here.dp, to)).start()

    def start(self):
        for dz, other in ROUND:
            self.start_to(dz, other)

    def finish_in(self):
        self.all.wait_recv()
        self.own.wait()

    def finish_out(self):
        self.all.wait_send()


def cols(start, width):
    return pl.ds(pl.multiple_of(start, 128), width)


def rows192(c):
    return pl.ds(pl.multiple_of(192 * c, 64), 192)


def rows48(pair):
    return pl.ds(pl.multiple_of(48 * pair, 16), 48)


def put_in_order(here, exchange, got, opens, hots, slots, out):
    for s in range(16):
        slots[s] = dot(opens[s], got[s]).astype(BF16)
    for dz, other in ROUND:
        pair = here.peer(dz, other)
        x = dot(hots[pair], slots[:, rows48(pair)].reshape(768, D))
        out[pair] = x.astype(BF16).reshape(2, TOK, D)
        exchange.start_to(dz, other)


def put_back(here, exchange, got, backs, hots_t, slots, out):
    for pair in range(8):
        x = dot(hots_t[pair], got[pair].reshape(384, D)).astype(BF16)
        slots[:, rows48(pair)] = x.reshape(16, 48, D)
    for i, step in enumerate(STEPS):
        s = here.at(*step)
        out[s] = dot(backs[s], slots[s]).astype(BF16)
        exchange.start_step(i)
    out[here.dp] = dot(backs[here.dp], slots[here.dp]).astype(BF16)
    exchange.own.start()


def tiles():
    for j in range(6):
        low = 0 if j < 4 else 512
        yield j, list(range(low, (j + 1) * TILE, TILE))


def allowed(j, k, end):
    diagonal, mixed = k == j * TILE, j >= 2 and k < 1024
    if not diagonal and not mixed:
        return None
    kp = k + iota((TILE, TILE), 0)
    qp = j * TILE + iota((1, TILE), 1)
    mask = None
    if mixed:
        mask = kp >= jnp.where(qp >= end, end, 0)
    if diagonal:
        causal = kp <= qp
        mask = causal if mask is None else mask & causal
    return mask


def forward_unit(e, end, q_ref, k_ref, vt_ref, o_ref, lse_ref):
    for j, ks in tiles():
        rows = slice(j * TILE, j * TILE + TILE)
        q = q_ref[e, rows]
        scores = []
        for k in ks:
            s = dot(k_ref[e, k : k + TILE], q, NT)
            mask = allowed(j, k, end)
            scores.append(s if mask is None else jnp.where(mask, s, -jnp.inf))
        top = jnp.max(functools.reduce(jnp.maximum, scores), axis=0, keepdims=True)
        expo = [jnp.exp2((s - top) * EXP2) for s in scores]
        total = jnp.sum(functools.reduce(jnp.add, expo), axis=0, keepdims=True)
        inverse = 1.0 / total
        att = jnp.zeros((D, TILE), F32)
        for k, x in zip(ks, expo):
            att += dot(vt_ref[e, :, k : k + TILE], (x * inverse).astype(BF16))
        o_ref[e, rows] = jnp.transpose(att).astype(BF16)
        lse_ref[e, :, rows] = top * EXP2 + jnp.log2(total)


def backward_unit(e, end, q_ref, d_ref, o_ref, lse_ref, k_ref, v_ref, kt_ref, gk_ref, gv_ref, gq_ref):
    for j, ks in tiles():
        rows = slice(j * TILE, j * TILE + TILE)
        q, d = q_ref[e, rows], d_ref[e, rows]
        product = d.astype(F32) * o_ref[e, rows].astype(F32)
        delta = jnp.sum(jnp.transpose(product), axis=0, keepdims=True)
        lse = lse_ref[e, :, rows]
        gq = jnp.zeros((D, TILE), F32)
        for k in ks:
            keys = slice(k, k + TILE)
            p = jnp.exp2(dot(k_ref[e, keys], q, NT) * EXP2 - lse)
            mask = allowed(j, k, end)
            if mask is not None:
                p = jnp.where(mask, p, 0.0)
            dp = dot(v_ref[e, keys], d, NT)
            ds = (p * (dp - delta)).astype(BF16)
            gv_ref[e, keys] += dot(p.astype(BF16), d)
            gk_ref[e, keys] += dot(ds, q)
            gq += dot(kt_ref[e, :, keys], ds)
        gq_ref[e, rows] = jnp.transpose(gq * SCALE).astype(BF16)


def whole_kernel(lengths_ref, row_ref, k_ref, v_ref, q_ref, d_ref, oo_ref, oq_ref, ok_ref, ov_ref,
                 info, infos, place, opens, backs, hots, hots_t, slots, got, sent, here_in, here_out, back, ready,
                 kt, vt, lse, gk, gv, parts, *sems):
    here = Here()
    p = here.dp
    sems = [sems[3 * i : 3 * i + 3] for i in range(28)]

    def head_of(ref, h):
        return lambda t: ref.at[:, cols(t * 256 + h * D, D)]

    def kv_head_of(ref):
        return lambda t: ref.at[:, cols((t // 4) * D, D)]

    inward = [kv_head_of(k_ref), kv_head_of(v_ref), head_of(q_ref, 0), head_of(d_ref, 0), head_of(q_ref, 1), head_of(d_ref, 1)]
    p_info = Plane(here, lambda t: info, lambda t: infos.at[t], infos.at[pl.ds(0, 15)], sems[24])
    p_in = [Plane(here, inward[n], lambda t, n=n: got.at[n, t], got.at[n, pl.ds(0, 15)], sems[n]) for n in range(6)]
    c_in = [
        Column(here, lambda c, n=n: sent.at[n, c], lambda c, n=n: here_in.at[n, :, rows192(c)],
               here_in.at[n, :, pl.ds(0, 7 * TOK)], sems[6 + n])
        for n in range(6)
    ]
    outward = [head_of(oo_ref, 0), head_of(oq_ref, 0), head_of(oo_ref, 1), head_of(oq_ref, 1)]
    outward += [lambda t: parts.at[0, t], lambda t: parts.at[1, t]]
    c_out = [
        Column(here, lambda c, n=n: here_out.at[n, :, rows192(c)], lambda c, n=n: back.at[n, c],
               back.at[n, pl.ds(0, 7)], sems[12 + n])
        for n in range(3)
    ]
    c_late = {
        (n, e): Column(here, lambda c, n=n, e=e: here_out.at[n, e, rows192(c)], lambda c, n=n, e=e: back.at[n, c, e],
                       back.at[n, pl.ds(0, 7), e], sems[15 + n - 3 if e == 0 else 25 + n - 3])
        for n in range(3, 6)
        for e in range(2)
    }
    spans = [ref.at[:, pl.ds(0, 15 * D)] for ref in (oo_ref, oq_ref, oo_ref, oq_ref)]
    spans += [parts.at[n, pl.ds(0, 15)] for n in range(2)]
    p_out = [Plane(here, lambda t, n=n: ready.at[n, t], outward[n], spans[n], sems[18 + n]) for n in range(6)]

    greet(here)
    p_in[0].start()
    dest_r = row_ref[...]
    g_r = group_of(dest_r)
    g_c = jnp.transpose(jnp.broadcast_to(g_r.astype(F32), (8, TOK)))[:, 0:1]
    same = (g_r.astype(F32) == g_c) & (iota((TOK, TOK), 0) < iota((TOK, TOK), 1))
    rank = jnp.sum(jnp.where(same, 1.0, 0.0), axis=0, keepdims=True).astype(jnp.int32)
    which = iota((8, TOK), 0)
    info[...] = jnp.where(
        which == 0,
        g_r * CAP + rank,
        jnp.where(which == 1, place_of(dest_r) + 1, jnp.where(which == 2, g_r >> 1, rank + CAP * (g_r & 1))),
    )

    p_info.start()
    p_in[1].start()
    p_in[2].start()

    p_info.finish_in()
    total = jnp.zeros((8, 768), F32)
    for s in range(16):
        opens[s] = jnp.where(iota((384, TOK), 0) == infos[s, 0:1], 1.0, 0.0).astype(BF16)
        named = jnp.where(iota((8, TOK), 0) == infos[s, 2:3], infos[s, 1:2].astype(F32), 0.0).astype(BF16)
        laned = jnp.where(iota((D, TOK), 0) == infos[s, 3:4], 1.0, 0.0).astype(BF16)
        mine = jnp.concatenate([dot(named, laned, NT), jnp.zeros((8, 640), F32)], axis=1)
        total += mine if s == 0 else pltpu.roll(mine, 48 * s, 1)
    odd = (iota((8, 768), 1) % 48) >= CAP
    place[...] = jnp.where(odd & (total > 0.0), total + 192.0, total)

    def hot_of(pair):
        return jnp.where(place[pair : pair + 1] == (iota((384, 768), 0) + 1).astype(F32), 1.0, 0.0)

    for pair in range(8):
        hots[pair] = hot_of(pair).astype(BF16)

    def order(n):
        p_in[n].finish_in()
        if n < 3:
            p_in[n + 3].start()
        put_in_order(here, c_in[n], got.at[n], opens, hots, slots, sent.at[n])

    order(0)
    order(1)
    slot_c = jnp.transpose(jnp.concatenate([infos[s, 0:1].astype(F32) for s in range(16)], axis=0))
    for s in range(16):
        backs[s] = jnp.where(iota((TOK, 384), 1).astype(F32) == slot_c[:, s : s + 1], 1.0, 0.0).astype(BF16)
    order(2)
    place_c = jnp.transpose(place[...])
    for pair in range(8):
        slot_of = (iota((768, 384), 1) + 1).astype(F32) == place_c[:, pair : pair + 1]
        hots_t[pair] = jnp.where(slot_of, 1.0, 0.0).astype(BF16)
    order(3)
    for n, turned in enumerate((kt, vt)):
        c_in[n].finish_in()
        for e in range(2):
            turned[e] = jnp.transpose(here_in[n, e].astype(F32)).astype(BF16)
    gk[...] = jnp.zeros_like(gk)
    gv[...] = jnp.zeros_like(gv)

    def end_of(e):
        return lengths_ref[0, 2 * here.ctx + e]

    def forward(h):
        c_in[2 + 2 * h].finish_in()

        @pl.loop(0, 2)
        def _(e):
            forward_unit(e, end_of(e), here_in.at[2 + 2 * h], here_in.at[0], vt, here_out.at[2 * h], lse.at[h])

        c_out[2 * h].start()

    def backward(h, e):
        backward_unit(e, end_of(e), here_in.at[2 + 2 * h], here_in.at[3 + 2 * h], here_out.at[2 * h], lse.at[h],
                      here_in.at[0], here_in.at[1], kt, gk, gv, here_out.at[1 + 2 * h])

        if h == 1:
            c_late[3, e].start()
            here_out[4, e] = (gk[e] * SCALE).astype(BF16)
            c_late[4, e].start()
            here_out[5, e] = gv[e].astype(BF16)
            c_late[5, e].start()

    def restore(n):
        for c in [c_out[n]] if n < 3 else [c_late[n, 0], c_late[n, 1]]:
            c.finish_in()
        put_back(here, p_out[n], back.at[n], backs, hots_t, slots, ready.at[n])

    forward(0)
    order(4)
    c_in[3].finish_in()
    backward(0, 0)
    order(5)
    backward(0, 1)
    c_out[1].start()
    restore(0)
    forward(1)
    c_in[5].finish_in()
    backward(1, 0)
    restore(1)
    backward(1, 1)
    for n in (2, 3, 4, 5):
        restore(n)
    for x in [p_info] + p_in + c_in + c_out + list(c_late.values()) + p_out[:4]:
        x.finish_out()
    for x in p_out[:4]:
        x.finish_in()
    for n, out in enumerate((ok_ref, ov_ref)):
        p_out[4 + n].finish_in()
        for x in range(4):
            added = parts[n, 4 * x].astype(F32)
            for y in range(1, 4):
                added += parts[n, 4 * x + y].astype(F32)
            out[:, x * D : x * D + D] = added.astype(BF16)
    for x in p_out[4:]:
        x.finish_out()


def local(queries, keys, values, grad_out, destination, lengths):
    scratch = [
        ((8, TOK), jnp.int32), ((16, 8, TOK), jnp.int32), ((8, 768), F32),
        ((16, 384, TOK), BF16), ((16, TOK, 384), BF16), ((8, 384, 768), BF16), ((8, 768, 384), BF16), ((16, 384, D), BF16),
        ((6, 16, TOK, D), BF16), ((6, 8, 2, TOK, D), BF16), ((6, 2, 1536, D), BF16),
        ((6, 2, 1536, D), BF16), ((6, 8, 2, TOK, D), BF16), ((6, 16, TOK, D), BF16),
        ((2, D, 1536), BF16), ((2, D, 1536), BF16), ((2, 2, 1, 1536), F32),
        ((2, 1536, D), F32), ((2, 1536, D), F32), ((2, 16, TOK, D), BF16),
    ]
    results = pl.pallas_call(
        whole_kernel,
        out_shape=(
            jax.ShapeDtypeStruct((TOK, 4096), BF16),
            jax.ShapeDtypeStruct((TOK, 4096), BF16),
            jax.ShapeDtypeStruct((TOK, 512), BF16),
            jax.ShapeDtypeStruct((TOK, 512), BF16),
        ),
        in_specs=[SMEM, VMEM] + [HBM] * 4,
        out_specs=(HBM, HBM, VMEM, VMEM),
        scratch_shapes=[pltpu.VMEM(shape, dtype) for shape, dtype in scratch]
        + [DMA] * 84,
        compiler_params=pltpu.CompilerParams(collective_id=0, has_side_effects=True, vmem_limit_bytes=60 << 20),
        name="whole",
    )(lengths.T, destination.reshape(1, TOK), keys, values, queries, grad_out)
    return settle(*results)


def settle_kernel(*refs):
    ins, outs, held, (load, store) = refs[:4], refs[4:8], refs[8:12], refs[12:]
    parts = [(n, part) for n in range(4) for part in range(4)]
    loads, stores = [], []
    for n, part in parts:
        rows = pl.ds(part * (TOK // 4), TOK // 4)
        loads.append(pltpu.make_async_copy(ins[n].at[rows], held[n].at[rows], load.at[n, part]))
        stores.append(pltpu.make_async_copy(held[n].at[rows], outs[n].at[rows], store.at[n, part]))
    for c in loads:
        c.start()
    for first, second in zip(loads, stores):
        first.wait()
        second.start()
    for c in stores:
        c.wait()


def settle(*results):
    return pl.pallas_call(
        settle_kernel,
        out_shape=tuple(jax.ShapeDtypeStruct(x.shape, x.dtype) for x in results),
        in_specs=[HBM] * 4,
        out_specs=(HBM,) * 4,
        scratch_shapes=[pltpu.VMEM(x.shape, x.dtype) for x in results] + [DMA((4, 4)), DMA((4, 4))],
        compiler_params=pltpu.CompilerParams(vmem_limit_bytes=60 << 20),
        name="settle",
    )(*results)


def solution(mesh):
    rows = P(("dp", "ctx"), None)
    return jax.shard_map(
        local,
        mesh=mesh,
        in_specs=(rows, rows, rows, rows, P(("dp", "ctx")), P()),
        out_specs=(rows, rows, rows, rows),
        check_vma=False,
    )
```
